32 devices in a mesh: groups: 2 (over x), tile: 16 (over z, y, core).
Axes of the slice: x: 2, y: 2, z: 4, core: 2. Of those that a mesh axis runs over, the one named last changes fastest.
Arguments:
- probes: float32 [8, 262144], P(None, ('groups', 'tile')), parts along dimension 1, may hold values from -6 to 6
- level_set: float32 [262144], P(('groups', 'tile')), parts along dimension 0, may hold values from -6 to 6
- unit_label: int32 [262144], P(('groups', 'tile')), parts along dimension 0, may hold values from 0 to 3
- contrast: float32 [8], P('groups'), parts along dimension 0, may hold values from 0.2 to 1.5
- station_weight: float32 [65536], P('groups'), parts along dimension 0, may hold values from 0.2 to 2
- u_factor: bfloat16 [4096, 32, 512], P(('groups', 'tile')), parts along dimension 0, may hold values from -1 to 1
- v_factor: bfloat16 [4096, 32, 512], P(('groups', 'tile')), parts along dimension 0, may hold values from -0.25 to 0.25
- col_owner: int32 [4096, 1], P('groups'), parts along dimension 0, may hold values from 0 to 15; in each aligned block of 128 rows (0 to 127, 128 to 255, ...) at most 16 rows name the same one
- col_local: int32 [4096], P('groups'), parts along dimension 0, may hold values from 0 to 15
- row_owner: int32 [4096, 1], P('groups'), parts along dimension 0, may hold values from 0 to 15; in each aligned block of 128 rows (0 to 127, 128 to 255, ...) at most 16 rows name the same one
- row_local: int32 [4096], P('groups'), parts along dimension 0, may hold values from 0 to 3
- tile_rank: int32 [4096], P('groups'), parts along dimension 0, may hold values from 8 to 32
Outputs:
- hessian_probes: float32 [8, 262144], P(None, ('groups', 'tile')), parts along dimension 1
The draws below stay inside these ranges and needn't reach their ends.
There are 2 independent parts, one for each index of `groups`. The reference program is written for one: setup_inputs(seed, part) draws one part's arguments, and reference() takes and returns one part's arrays. A program takes and returns all parts, laid end to end along the dimension named above; each array names one. Nothing has to cross between parts.
Inputs may be any that keep to these rules, and one draw needn't show every extreme that they name: `col_owner`: among the 128 tiles of one device (aligned blocks of 128 entries) no owner is named more than 16 times, a bound that some block reaches. `row_owner`: among the 128 tiles of one device (aligned blocks of 128 entries) no owner is named more than 16 times, a bound that some block reaches.
All inputs are finite; a program needn't handle non-finite values.
Results may differ from the reference program's by a relative error of at most 0.005.
Values may be sent and summed in bfloat16 or wider, within the bound.
A program may use at most 64 MiB of HBM per device.

```python
import math
import jax
import jax.numpy as jnp
import numpy as np
from jax import lax

PROBES = 8
RANK = 32
CELL_BLOCK = 512
STATION_BLOCK = 512
UNITS = 4
CB_DEV = 16
SB_DEV = 4
TILE_DEV = 128
CAP = 16
NCB = 256
NSB = 64
CELLS = 131072
STATIONS = 32768
TILES = 2048
N_TILE = 16


def place_ends(drawn, rng, smallest, top_value):
    longest = drawn.shape.index(max(drawn.shape))
    spots = []
    for shift in (0, 1):
        where = [jax.random.randint(jax.random.fold_in(rng, axis), (), 0, length) for axis, length in enumerate(drawn.shape)]
        where[longest] = (where[longest] + shift) % drawn.shape[longest]
        spots.append(tuple(where))
    return drawn.at[spots[0]].set(smallest).at[spots[1]].set(top_value)


def steps_of(rng, dims, split, least, high):
    gain, own = 1.0, jax.random.fold_in(rng, 6)
    for position, blocks in split:
        steps = jnp.exp(jax.random.uniform(jax.random.fold_in(own, position), (blocks,), jnp.float32, least / len(split), high / len(split)))
        gain = gain * jnp.repeat(steps, dims[position] // blocks).reshape([-1 if axis == position else 1 for axis in range(len(dims))])
    return gain


def routed_block(rng, own, number, rows, amount, top, most, skew):
    ranking = jax.random.permutation(rng, amount)
    heavy_load, ordinary = shares(amount, rows * top, most, skew, True), shares(amount, rows * top, most, skew, False)
    places = jnp.arange(amount)

    def named(tallies, offset_by):
        used = int((tallies > 0).sum())
        fixed = max(1, used // 4)
        passed = fixed + (places - fixed + offset_by * (used - fixed)) % max(1, amount - fixed)
        return jnp.zeros((amount,), jnp.int32).at[ranking[jnp.where(places < fixed, places, passed)]].set(jnp.asarray(tallies, jnp.int32))

    tallies = jnp.where(number % 4 == 0, named(heavy_load, number // 4), named(ordinary, number - number // 4 - 1))
    mixed = jax.random.permutation(jax.random.fold_in(own, 3), amount)
    source_of, sink = mixed[0:amount // 2 * 2:2], mixed[1:amount // 2 * 2:2]
    margin = jnp.minimum(tallies[source_of] - 1, most - tallies[sink]) // 2
    margin = jnp.where((source_of == ranking[0]) | (sink == ranking[0]) | (tallies[sink] == 0), 0, jnp.maximum(margin, 0))
    passed = jax.random.randint(jax.random.fold_in(own, 4), (amount // 2,), 0, 1 << 20) % (margin + 1)
    tallies = tallies.at[source_of].add(-passed).at[sink].add(passed)
    members = jnp.searchsorted(jnp.cumsum(tallies), jnp.arange(rows * top), side="right").astype(jnp.int32)
    table = members.reshape(top, rows).T
    table = table[jax.random.permutation(jax.random.fold_in(own, 1), rows)]
    offset_by = jax.random.randint(jax.random.fold_in(own, 2), (rows, 1), 0, top)
    return jnp.take_along_axis(table, (jnp.arange(top)[None, :] + offset_by) % top, axis=1)


def shares(number_of, total, reach, lean, full):
    weights = [(1 << 20) // math.isqrt(standing ** lean) + 1 for standing in range(1, number_of + 1)]
    largest = reach if full else min(reach, max(-(-total // number_of), total * weights[0] // sum(weights)))
    least = 1 if total - largest >= number_of - 1 else 0
    holding, surplus = [largest] + [least] * (number_of - 1), total - largest - least * (number_of - 1)
    while surplus > 0:
        movable = [i for i in range(1, number_of) if holding[i] < largest] or [i for i in range(1, number_of) if holding[i] < reach]
        pool, left = sum([weights[i] for i in movable]), surplus
        for i in movable:
            addition = min(reach - holding[i], max(1, left * weights[i] // pool), surplus)
            holding[i] = holding[i] + addition
            surplus = surplus - addition
    return np.array(holding)


def noise(stream_key, shape, width, reach, split=(), kind=jnp.bfloat16):
    values = width * jax.random.normal(stream_key, shape, jnp.float32)
    if split:
        values = values * steps_of(stream_key, shape, split, -0.22, 0.18)
    return jnp.clip(values, -reach, reach).astype(kind)


def setup_inputs(seed: int = 0, part: int = 0) -> dict:
    streams_of = jax.random.split(jax.random.key(seed), 13)
    part_splits = jax.random.split(jax.random.fold_in(streams_of[12], part), 13)
    probes = noise(part_splits[0], (PROBES, CELLS), 1.0, 6.0, ((1, 16),), jnp.float32)
    level_set = noise(part_splits[1], (CELLS,), 1.0, 6.0, ((0, 16),), jnp.float32)
    unit_label = place_ends(jax.random.randint(part_splits[2], (CELLS,), 0, UNITS), jax.random.fold_in(part_splits[2], 1), 0, UNITS - 1).astype(jnp.int32)
    contrast = jnp.clip(jnp.exp(jax.random.uniform(part_splits[3], (UNITS,), jnp.float32, math.log(0.2), math.log(1.5))), 0.2, 1.5)
    station_weight = jnp.clip(jnp.exp(jax.random.uniform(part_splits[4], (STATIONS,), jnp.float32, math.log(0.2), math.log(2.0))), 0.2, 2.0)
    u_factor = noise(part_splits[5], (TILES, RANK, STATION_BLOCK), RANK ** -0.5, 1.0, ((0, 16),))
    v_factor = noise(part_splits[6], (TILES, RANK, CELL_BLOCK), CELL_BLOCK ** -0.5, 0.25, ((0, 16),))
    col_owner_keys = jax.random.split(jax.random.fold_in(part_splits[7], 1), TILES // TILE_DEV)
    col_owner_turns = jax.random.permutation(jax.random.fold_in(part_splits[7], 3), TILES // TILE_DEV)
    col_owner = jax.vmap(lambda own, number: routed_block(jax.random.fold_in(part_splits[7], 2), own, number, TILE_DEV, N_TILE, 1, CAP, 2))(col_owner_keys, col_owner_turns).reshape((TILES, 1))
    col_local = place_ends(jax.random.randint(part_splits[8], (TILES,), 0, CB_DEV), jax.random.fold_in(part_splits[8], 1), 0, CB_DEV - 1).astype(jnp.int32)
    row_owner_keys = jax.random.split(jax.random.fold_in(part_splits[9], 1), TILES // TILE_DEV)
    row_owner_turns = jax.random.permutation(jax.random.fold_in(part_splits[9], 3), TILES // TILE_DEV)
    row_owner = jax.vmap(lambda own, number: routed_block(jax.random.fold_in(part_splits[9], 2), own, number, TILE_DEV, N_TILE, 1, CAP, 2))(row_owner_keys, row_owner_turns).reshape((TILES, 1))
    row_local = place_ends(jax.random.randint(part_splits[10], (TILES,), 0, SB_DEV), jax.random.fold_in(part_splits[10], 1), 0, SB_DEV - 1).astype(jnp.int32)
    tile_rank = place_ends(jax.random.randint(part_splits[11], (TILES,), RANK // 4, RANK + 1), jax.random.fold_in(part_splits[11], 1), RANK // 4, RANK).astype(jnp.int32)
    return {"probes": probes, "level_set": level_set, "unit_label": unit_label, "contrast": contrast, "station_weight": station_weight, "u_factor": u_factor, "v_factor": v_factor, "col_owner": col_owner, "col_local": col_local, "row_owner": row_owner, "row_local": row_local, "tile_rank": tile_rank}


def forward_tiles(operands):
    cells, v_part, u_part, keep_part = operands
    coeff = jnp.einsum('tkc,trc->tkr', cells.astype(jnp.float32), v_part.astype(jnp.float32))
    coeff = (coeff * keep_part).astype(jnp.bfloat16)
    return jnp.einsum('tkr,trs->tks', coeff.astype(jnp.float32), u_part.astype(jnp.float32))


def adjoint_tiles(operands):
    data, v_part, u_part, keep_part = operands
    back = jnp.einsum('tks,trs->tkr', data.astype(jnp.float32), u_part.astype(jnp.float32))
    back = (back * keep_part).astype(jnp.bfloat16)
    return jnp.einsum('tkr,trc->tkc', back.astype(jnp.float32), v_part.astype(jnp.float32))


def grouped(array):
    return array.reshape((N_TILE, TILE_DEV) + array.shape[1:])


def reference(probes, level_set, unit_label, contrast, station_weight, u_factor, v_factor, col_owner, col_local, row_owner, row_local, tile_rank):
    scaling = contrast[unit_label] / (1.0 + level_set * level_set)
    scaled = (probes * scaling[None, :]).astype(jnp.bfloat16)
    cell_rows = scaled.reshape(PROBES, NCB, CELL_BLOCK).transpose(1, 0, 2)
    col_global = (col_owner[:, 0] * CB_DEV + col_local).astype(jnp.int32)
    row_global = (row_owner[:, 0] * SB_DEV + row_local).astype(jnp.int32)
    keep = (jnp.arange(RANK, dtype=jnp.int32)[None, :] < tile_rank[:, None]).astype(jnp.float32)[:, None, :]
    tile_cells = cell_rows[col_global]
    partial_value = lax.map(forward_tiles, (grouped(tile_cells), grouped(v_factor), grouped(u_factor), grouped(keep)))
    predicted = jax.ops.segment_sum(partial_value.reshape(TILES, PROBES, STATION_BLOCK), row_global, num_segments=NSB)
    weighted = (predicted * station_weight.reshape(NSB, 1, STATION_BLOCK)).astype(jnp.bfloat16)
    tile_data = weighted[row_global]
    spread = lax.map(adjoint_tiles, (grouped(tile_data), grouped(v_factor), grouped(u_factor), grouped(keep)))
    summed = jax.ops.segment_sum(spread.reshape(TILES, PROBES, CELL_BLOCK), col_global, num_segments=NCB)
    gradient = summed.transpose(1, 0, 2).reshape(PROBES, CELLS)
    return scaling[None, :] * gradient
```

```python
import functools

import jax
import jax.numpy as jnp
from jax import lax
from jax.experimental import pallas as pl
from jax.experimental.pallas import tpu as pltpu
from jax.sharding import PartitionSpec as P

MESH = pl.DeviceIdType.MESH
VMEM_LIMIT = 56 * 1024 * 1024
GROUP = 8
F32 = jnp.float32
BF16 = jnp.bfloat16


def place(lines):
    me = lax.axis_index("tile")
    core = lax.rem(me, 2)
    side = lax.rem(me // 2, 2)
    step = me // 4
    return me, core, side, step


def index_of(step, side, core):
    return (step * 2 + side) * 2 + core


def enter(lines, step, side, core):
    barrier = pltpu.get_barrier_semaphore()
    for d in range(1, lines):
        peer = index_of(lax.rem(step + d, lines), side, core)
        pl.semaphore_signal(barrier, inc=1, device_id={"tile": peer}, device_id_type=MESH)
    for peer in (index_of(step, 1 - side, core), index_of(step, side, 1 - core)):
        pl.semaphore_signal(barrier, inc=1, device_id={"tile": peer}, device_id_type=MESH)
    pl.semaphore_wait(barrier, lines + 1)


def remote(src, dst, send, recv, peer):
    return pltpu.make_async_remote_copy(
        src_ref=src,
        dst_ref=dst,
        send_sem=send,
        recv_sem=recv,
        device_id={"tile": peer},
        device_id_type=MESH,
    )


def gather_shards(lines, own, out, local_sem, sems, step, side, core):
    send_z, recv_z, send_y, recv_y, send_c, recv_c = sems
    me = index_of(step, side, core)
    across = index_of(step, 1 - side, core)
    twin = index_of(step, side, 1 - core)
    started = []

    def go(src, slot, send, recv, peer):
        copy = remote(src, out.at[slot], send, recv, peer)
        copy.start()
        started.append(copy)

    go(own, me, send_y.at[0], recv_y.at[0], across)
    for d in range(1, lines):
        peer = index_of(lax.rem(step + d, lines), side, core)
        go(own, me, send_z.at[d - 1], recv_z.at[d - 1], peer)
    go(own, me, send_c.at[0], recv_c.at[0], twin)
    mine = pltpu.make_async_copy(own, out.at[me], local_sem)
    mine.start()

    def arrived(slot, recv, peer):
        remote(out.at[slot], out.at[slot], recv, recv, peer).wait_recv()

    for k in range(lines + 1):
        if 1 <= k < lines:
            slot = index_of(lax.rem(step + lines - k, lines), side, core)
            arrived(slot, recv_z.at[k - 1], me)
            go(out.at[slot], slot, send_y.at[k], recv_y.at[k], across)
            go(out.at[slot], slot, send_c.at[k], recv_c.at[k], twin)
        if k >= 1:
            j = k - 1
            slot = index_of(lax.rem(step + lines - j, lines), 1 - side, core)
            arrived(slot, recv_y.at[j], across)
            go(out.at[slot], slot, send_c.at[lines + j], recv_c.at[lines + j], twin)
    for k in range(lines):
        for far in range(2):
            where = 1 - side if far else side
            slot = index_of(lax.rem(step + lines - k, lines), where, 1 - core)
            arrived(slot, recv_c.at[far * lines + k], twin)
    mine.wait()
    for copy in started:
        copy.wait_send()


def gather_sems(lines):
    dma = pltpu.SemaphoreType.DMA
    return [
        dma((lines - 1,)),
        dma((lines - 1,)),
        dma((lines,)),
        dma((lines,)),
        dma((2 * lines,)),
        dma((2 * lines,)),
    ]


def cell_scaling(level, label, contrast, units):
    picked = jnp.full(level.shape, contrast[0], F32)
    for unit in range(1, units):
        picked = jnp.where(label == unit, contrast[unit], picked)
    return picked / (1.0 + level * level)


def halves(block):
    half = block.shape[1] // 2
    return jnp.concatenate([block[:, :half], block[:, half:]], axis=0)


def cells_kernel(lines, units, contrast, probes, level, label, out, own, local_sem, *sems):
    _, core, side, step = place(lines)
    enter(lines, step, side, core)
    count = own.shape[0]
    width = probes.shape[1] // count
    for b in range(count):
        cut = pl.ds(b * width, width)
        scaling = cell_scaling(level[:, cut], label[:, cut], contrast, units)
        own[b] = halves(probes[:, cut] * scaling).astype(BF16)
    gather_shards(lines, own, out, local_sem, sems, step, side, core)


def tiles_kernel(
    per_step, rank_max, take, put, ranks, held, first, second, out, total
):
    i = pl.program_id(0)

    @pl.when(i == 0)
    def _():
        total[...] = jnp.zeros_like(total)

    rows = GROUP * rank_max
    lane = lax.broadcasted_iota(jnp.int32, (8, rows), 1)
    for g in range(per_step // GROUP):
        pieces = []
        for j in range(GROUP):
            block = held[take[i * per_step + g * GROUP + j]].astype(F32)
            pieces.append(jnp.concatenate([block[:8], block[8:]], axis=1))
        data = jnp.concatenate(pieces, axis=0).astype(BF16)
        inner = lax.dot_general(
            data,
            first[g * rows : (g + 1) * rows],
            (((1,), (1,)), ((), ())),
            preferred_element_type=F32,
        )
        kept = []
        for j in range(GROUP):
            start = j * rank_max
            end = start + ranks[i * per_step + g * GROUP + j]
            part = inner[j * 8 : (j + 1) * 8]
            kept.append(jnp.where((lane >= start) & (lane < end), part, 0.0))
        coeff = jnp.concatenate(kept, axis=0).astype(BF16)
        result = jnp.dot(
            coeff, second[g * rows : (g + 1) * rows], preferred_element_type=F32
        )
        for j in range(GROUP):
            spot = put[i * per_step + g * GROUP + j]
            total[spot] += result[j * 8 : (j + 1) * 8]

    @pl.when(i == pl.num_programs(0) - 1)
    def _():
        out[...] = total[...].reshape(out.shape).astype(out.dtype)


def apply_tiles(take, put, ranks, held, first, second, blocks, dtype, rank_max):
    tiles = take.shape[0]
    per_step = 2 * GROUP
    width = second.shape[1]
    rows = per_step * rank_max
    spec = pl.BlockSpec((rows, width), lambda i, *_: (i, 0))
    return pl.pallas_call(
        functools.partial(tiles_kernel, per_step, rank_max),
        out_shape=jax.ShapeDtypeStruct((blocks * 8, width), dtype),
        grid_spec=pltpu.PrefetchScalarGridSpec(
            num_scalar_prefetch=3,
            grid=(tiles // per_step,),
            in_specs=[
                pl.BlockSpec(held.shape, lambda i, *_: (0, 0, 0)),
                spec,
                spec,
            ],
            out_specs=pl.BlockSpec((blocks * 8, width), lambda i, *_: (0, 0)),
            scratch_shapes=[pltpu.VMEM((blocks, 8, width), F32)],
        ),
        compiler_params=pltpu.CompilerParams(vmem_limit_bytes=VMEM_LIMIT),
        cost_estimate=pl.CostEstimate(
            flops=4 * tiles * GROUP * 8 * rank_max * width,
            bytes_accessed=4 * tiles * rank_max * width,
            transcendentals=0,
        ),
    )(take, put, ranks, held, first, second)


def stations_kernel(
    lines, weight, part, out,
    got_c, far_sum, got_y, near_sum, send_line, got_z, own,
    c_send, c_recv, y_send, y_recv, z_send, z_recv, local_sem, *sems
):
    me, core, side, step = place(lines)
    across = index_of(step, 1 - side, core)
    twin = index_of(step, side, 1 - core)
    enter(lines, step, side, core)
    run = part.shape[0] // 4
    chunk = run // lines

    def band(c, y):
        return pl.ds(pl.multiple_of((c * 2 + y) * run, run), run)

    copies = []
    for far in range(2):
        y = 1 - side if far == 0 else side
        copy = remote(
            part.at[band(1 - core, y)], got_c.at[far], c_send.at[far], c_recv.at[far], twin
        )
        copy.start()
        copies.append(copy)
    copies[0].wait_recv()
    far_sum[...] = (part[band(core, 1 - side)] + got_c[0]).astype(BF16)
    y_copy = remote(far_sum, got_y, y_send, y_recv, across)
    y_copy.start()
    copies[1].wait_recv()
    near_sum[...] = part[band(core, side)] + got_c[1]
    y_copy.wait_recv()
    z_copies = []
    for d in range(1, lines):
        there = lax.rem(step + d, lines)
        cut = pl.ds(pl.multiple_of(there * chunk, chunk), chunk)
        send_line[d - 1] = (near_sum[cut] + got_y[cut].astype(F32)).astype(BF16)
        copy = remote(
            send_line.at[d - 1], got_z.at[d - 1], z_send.at[d - 1], z_recv.at[d - 1],
            index_of(there, side, core),
        )
        copy.start()
        z_copies.append(copy)
    cut = pl.ds(pl.multiple_of(step * chunk, chunk), chunk)
    total = near_sum[cut] + got_y[cut].astype(F32)
    for d in range(1, lines):
        z_copies[d - 1].wait_recv()
        total += got_z[d - 1].astype(F32)
    count = own.shape[0]
    width = part.shape[1]
    for b in range(count):
        start = pl.multiple_of(me * (count * width) + b * width, width)
        factor = weight[:, pl.ds(start, width)]
        own[b] = halves(total[b * 8 : (b + 1) * 8] * factor).astype(BF16)
    gather_shards(lines, own, out, local_sem, sems, step, side, core)
    for copy in copies + [y_copy] + z_copies:
        copy.wait_send()


def back_kernel(
    lines, units, contrast, level, label, part, out,
    got_c, send_y, got_y, send_z, got_z,
    c_send, c_recv, y_send, y_recv, z_send, z_recv
):
    _, core, side, step = place(lines)
    across = index_of(step, 1 - side, core)
    twin = index_of(step, side, 1 - core)
    enter(lines, step, side, core)
    chunk = part.shape[0] // (4 * lines)

    def band(c, y, z):
        return pl.ds(pl.multiple_of(((c * 2 + y) * lines + z) * chunk, chunk), chunk)

    def target(k):
        return lax.rem(step + k + 1, lines)

    c_copies = [[None] * lines, [None] * lines]
    for k in range(lines):
        for far in range(2):
            y = 1 - side if far == 0 else side
            copy = remote(
                part.at[band(1 - core, y, target(k))],
                got_c.at[far, k],
                c_send.at[far, k],
                c_recv.at[far, k],
                twin,
            )
            copy.start()
            c_copies[far][k] = copy
    y_copies = []
    for k in range(lines):
        c_copies[0][k].wait_recv()
        send_y[k] = (
            part[band(core, 1 - side, target(k))].astype(F32) + got_c[0, k].astype(F32)
        ).astype(BF16)
        copy = remote(send_y.at[k], got_y.at[k], y_send.at[k], y_recv.at[k], across)
        copy.start()
        y_copies.append(copy)
    z_copies = []
    total = None
    for k in range(lines):
        c_copies[1][k].wait_recv()
        y_copies[k].wait_recv()
        value = (
            part[band(core, side, target(k))].astype(F32)
            + got_c[1, k].astype(F32)
            + got_y[k].astype(F32)
        )
        if k < lines - 1:
            send_z[k] = value.astype(BF16)
            copy = remote(
                send_z.at[k], got_z.at[k], z_send.at[k], z_recv.at[k],
                index_of(target(k), side, core),
            )
            copy.start()
            z_copies.append(copy)
        else:
            total = value
    for copy in z_copies:
        copy.wait_recv()
    width = part.shape[1]
    for b in range(chunk // 8):
        rows = slice(b * 8, (b + 1) * 8)
        cut = pl.ds(b * width, width)
        piece = total[rows]
        for k in range(lines - 1):
            piece += got_z[k, b * 8 : (b + 1) * 8].astype(F32)
        out[:, cut] = piece * cell_scaling(level[:, cut], label[:, cut], contrast, units)
    for copy in c_copies[0] + c_copies[1] + y_copies + z_copies:
        copy.wait_send()


def params(number):
    return pltpu.CompilerParams(
        collective_id=number, has_side_effects=True, vmem_limit_bytes=VMEM_LIMIT
    )


VM = pl.BlockSpec(memory_space=pltpu.VMEM)
SM = pl.BlockSpec(memory_space=pltpu.SMEM)
ANY = pl.BlockSpec(memory_space=pl.ANY)


def shards(
    probes,
    level_set,
    unit_label,
    contrast,
    station_weight,
    u_factor,
    v_factor,
    col_owner,
    col_local,
    row_owner,
    row_local,
    tile_rank,
):
    peers = lax.axis_size("tile")
    lines = peers // 4
    own_index = lax.axis_index("tile")
    tiles, rank_max, width = u_factor.shape
    cell_total = probes.shape[1]
    cell_blocks = cell_total // width
    station_blocks = station_weight.shape[0] // (peers * width)
    units = contrast.shape[0]
    half = width // 2
    dma = pltpu.SemaphoreType.DMA

    def own_part(table):
        return lax.dynamic_slice_in_dim(table.reshape(-1), own_index * tiles, tiles)

    def places(owner, local, blocks):
        owner, local = own_part(owner), own_part(local)
        moved = (owner % 2 * 2 + owner // 2 % 2) * lines + owner // 4
        return owner * blocks + local, moved * blocks + local

    col_take, col_put = places(col_owner, col_local, cell_blocks)
    row_take, row_put = places(row_owner, row_local, station_blocks)
    ranks = own_part(tile_rank)
    u_rows = u_factor.reshape(tiles * rank_max, width)
    v_rows = v_factor.reshape(tiles * rank_max, width)
    level = level_set.reshape(1, cell_total)
    label = unit_label.reshape(1, cell_total)
    weight = station_weight.reshape(1, -1)

    with jax.named_scope("gather_cells"):
        cells = pl.pallas_call(
            functools.partial(cells_kernel, lines, units),
            out_shape=jax.ShapeDtypeStruct((peers, cell_blocks, 16, half), BF16),
            in_specs=[SM, VM, VM, VM],
            out_specs=ANY,
            scratch_shapes=[pltpu.VMEM((cell_blocks, 16, half), BF16), dma]
            + gather_sems(lines),
            compiler_params=params(0),
        )(contrast, probes, level, label)

    with jax.named_scope("forward_tiles"):
        partial = apply_tiles(
            col_take, row_put, ranks, cells.reshape(-1, 16, half), v_rows, u_rows,
            peers * station_blocks, F32, rank_max,
        )

    run = lines * station_blocks * 8
    chunk = station_blocks * 8
    with jax.named_scope("sum_stations"):
        data = pl.pallas_call(
            functools.partial(stations_kernel, lines),
            out_shape=jax.ShapeDtypeStruct((peers, station_blocks, 16, half), BF16),
            in_specs=[VM, VM],
            out_specs=ANY,
            scratch_shapes=[
                pltpu.VMEM((2, run, width), F32),
                pltpu.VMEM((run, width), BF16),
                pltpu.VMEM((run, width), BF16),
                pltpu.VMEM((run, width), F32),
                pltpu.VMEM((lines - 1, chunk, width), BF16),
                pltpu.VMEM((lines - 1, chunk, width), BF16),
                pltpu.VMEM((station_blocks, 16, half), BF16),
                dma((2,)),
                dma((2,)),
                dma,
                dma,
                dma((lines - 1,)),
                dma((lines - 1,)),
                dma,
            ]
            + gather_sems(lines),
            compiler_params=params(1),
        )(weight, partial)

    with jax.named_scope("adjoint_tiles"):
        spread = apply_tiles(
            row_take, col_put, ranks, data.reshape(-1, 16, half), u_rows, v_rows,
            peers * cell_blocks, BF16, rank_max,
        )

    chunk = cell_blocks * 8
    with jax.named_scope("sum_cells"):
        return pl.pallas_call(
            functools.partial(back_kernel, lines, units),
            out_shape=jax.ShapeDtypeStruct(probes.shape, F32),
            in_specs=[SM, VM, VM, VM],
            out_specs=VM,
            scratch_shapes=[
                pltpu.VMEM((2, lines, chunk, width), BF16),
                pltpu.VMEM((lines, chunk, width), BF16),
                pltpu.VMEM((lines, chunk, width), BF16),
                pltpu.VMEM((lines - 1, chunk, width), BF16),
                pltpu.VMEM((lines - 1, chunk, width), BF16),
                dma((2, lines)),
                dma((2, lines)),
                dma((lines,)),
                dma((lines,)),
                dma((lines - 1,)),
                dma((lines - 1,)),
            ],
            compiler_params=params(2),
        )(contrast, level, label, spread)


def solution(mesh):
    placed = (
        P(None, ("groups", "tile")),
        P(("groups", "tile")),
        P(("groups", "tile")),
        P("groups"),
        P("groups"),
        P(("groups", "tile"), None, None),
        P(("groups", "tile"), None, None),
        P("groups", None),
        P("groups"),
        P("groups", None),
        P("groups"),
        P("groups"),
    )
    return jax.shard_map(
        shards, mesh=mesh, in_specs=placed, out_specs=P(None, ("groups", "tile")), check_vma=False
    )
```

```python
import functools

import jax
import jax.numpy as jnp
from jax import lax
from jax.experimental import pallas as pl
from jax.experimental.pallas import tpu as pltpu
from jax.sharding import PartitionSpec as P

MESH = pl.DeviceIdType.MESH
VMEM_LIMIT = 56 * 1024 * 1024
GROUP = 8
F32 = jnp.float32
BF16 = jnp.bfloat16


def place(lines):
    me = lax.axis_index("tile")
    core = lax.rem(me, 2)
    side = lax.rem(me // 2, 2)
    step = me // 4
    return me, core, side, step


def index_of(step, side, core):
    return (step * 2 + side) * 2 + core


def enter(lines, step, side, core):
    barrier = pltpu.get_barrier_semaphore()
    for d in range(1, lines):
        peer = index_of(lax.rem(step + d, lines), side, core)
        pl.semaphore_signal(barrier, inc=1, device_id={"tile": peer}, device_id_type=MESH)
    for peer in (index_of(step, 1 - side, core), index_of(step, side, 1 - core)):
        pl.semaphore_signal(barrier, inc=1, device_id={"tile": peer}, device_id_type=MESH)
    pl.semaphore_wait(barrier, lines + 1)


def remote(src, dst, send, recv, peer):
    return pltpu.make_async_remote_copy(
        src_ref=src,
        dst_ref=dst,
        send_sem=send,
        recv_sem=recv,
        device_id={"tile": peer},
        device_id_type=MESH,
    )


def gather_shards(lines, own, out, local_sem, sems, step, side, core):
    send_z, recv_z, send_y, recv_y, send_c, recv_c = sems
    me = index_of(step, side, core)
    across = index_of(step, 1 - side, core)
    twin = index_of(step, side, 1 - core)
    started = []

    def go(src, slot, send, recv, peer):
        copy = remote(src, out.at[slot], send, recv, peer)
        copy.start()
        started.append(copy)

    go(own, me, send_y.at[0], recv_y.at[0], across)
    for d in range(1, lines):
        peer = index_of(lax.rem(step + d, lines), side, core)
        go(own, me, send_z.at[d - 1], recv_z.at[d - 1], peer)
    go(own, me, send_c.at[0], recv_c.at[0], twin)
    mine = pltpu.make_async_copy(own, out.at[me], local_sem)
    mine.start()

    def arrived(slot, recv, peer):
        remote(out.at[slot], out.at[slot], recv, recv, peer).wait_recv()

    for k in range(lines + 1):
        if 1 <= k < lines:
            slot = index_of(lax.rem(step + lines - k, lines), side, core)
            arrived(slot, recv_z.at[k - 1], me)
            go(out.at[slot], slot, send_y.at[k], recv_y.at[k], across)
            go(out.at[slot], slot, send_c.at[k], recv_c.at[k], twin)
        if k >= 1:
            j = k - 1
            slot = index_of(lax.rem(step + lines - j, lines), 1 - side, core)
            arrived(slot, recv_y.at[j], across)
            go(out.at[slot], slot, send_c.at[lines + j], recv_c.at[lines + j], twin)
    for k in range(lines):
        for far in range(2):
            where = 1 - side if far else side
            slot = index_of(lax.rem(step + lines - k, lines), where, 1 - core)
            arrived(slot, recv_c.at[far * lines + k], twin)
    mine.wait()
    for copy in started:
        copy.wait_send()


def gather_sems(lines):
    dma = pltpu.SemaphoreType.DMA
    return [
        dma((lines - 1,)),
        dma((lines - 1,)),
        dma((lines,)),
        dma((lines,)),
        dma((2 * lines,)),
        dma((2 * lines,)),
    ]


def cell_scaling(level, label, contrast, units):
    picked = jnp.full(level.shape, contrast[0], F32)
    for unit in range(1, units):
        picked = jnp.where(label == unit, contrast[unit], picked)
    return picked / (1.0 + level * level)


def halves(block):
    half = block.shape[1] // 2
    return jnp.concatenate([block[:, :half], block[:, half:]], axis=0)


def cells_kernel(lines, units, contrast, probes, level, label, out, own, local_sem, *sems):
    _, core, side, step = place(lines)
    enter(lines, step, side, core)
    count = own.shape[0]
    width = probes.shape[1] // count
    for b in range(count):
        cut = pl.ds(b * width, width)
        scaling = cell_scaling(level[:, cut], label[:, cut], contrast, units)
        own[b] = halves(probes[:, cut] * scaling).astype(BF16)
    gather_shards(lines, own, out, local_sem, sems, step, side, core)


def tiles_kernel(
    per_step, rank_max, take, put, ranks, held, first, second, out, total
):
    i = pl.program_id(0)

    @pl.when(i == 0)
    def _():
        total[...] = jnp.zeros_like(total)

    rows = GROUP * rank_max
    lane = lax.broadcasted_iota(jnp.int32, (8, rows), 1)
    groups = range(per_step // GROUP)
    inners = []
    for g in groups:
        pieces = []
        for j in range(GROUP):
            block = held[take[i * per_step + g * GROUP + j]].astype(F32)
            pieces.append(jnp.concatenate([block[:8], block[8:]], axis=1))
        data = jnp.concatenate(pieces, axis=0).astype(BF16)
        inners.append(
            lax.dot_general(
                data,
                first[g * rows : (g + 1) * rows],
                (((1,), (1,)), ((), ())),
                preferred_element_type=F32,
            )
        )
    results = []
    for g in groups:
        kept = []
        for j in range(GROUP):
            start = j * rank_max
            end = start + ranks[i * per_step + g * GROUP + j]
            part = inners[g][j * 8 : (j + 1) * 8]
            kept.append(jnp.where((lane >= start) & (lane < end), part, 0.0))
        coeff = jnp.concatenate(kept, axis=0).astype(BF16)
        results.append(
            jnp.dot(coeff, second[g * rows : (g + 1) * rows], preferred_element_type=F32)
        )
    for g in groups:
        for j in range(GROUP):
            spot = put[i * per_step + g * GROUP + j]
            total[spot] += results[g][j * 8 : (j + 1) * 8]

    @pl.when(i == pl.num_programs(0) - 1)
    def _():
        out[...] = total[...].reshape(out.shape).astype(out.dtype)


def apply_tiles(take, put, ranks, held, first, second, blocks, dtype, rank_max):
    tiles = take.shape[0]
    per_step = 4 * GROUP
    width = second.shape[1]
    rows = per_step * rank_max
    spec = pl.BlockSpec((rows, width), lambda i, *_: (i, 0))
    return pl.pallas_call(
        functools.partial(tiles_kernel, per_step, rank_max),
        out_shape=jax.ShapeDtypeStruct((blocks * 8, width), dtype),
        grid_spec=pltpu.PrefetchScalarGridSpec(
            num_scalar_prefetch=3,
            grid=(tiles // per_step,),
            in_specs=[
                pl.BlockSpec(held.shape, lambda i, *_: (0, 0, 0)),
                spec,
                spec,
            ],
            out_specs=pl.BlockSpec((blocks * 8, width), lambda i, *_: (0, 0)),
            scratch_shapes=[pltpu.VMEM((blocks, 8, width), F32)],
        ),
        compiler_params=pltpu.CompilerParams(vmem_limit_bytes=VMEM_LIMIT),
        cost_estimate=pl.CostEstimate(
            flops=4 * tiles * GROUP * 8 * rank_max * width,
            bytes_accessed=4 * tiles * rank_max * width,
            transcendentals=0,
        ),
    )(take, put, ranks, held, first, second)


def stations_kernel(
    pairs, weight, part, out,
    got_c, send_line, got_line, own,
    c_send, c_recv, l_send, l_recv, a_send, a_recv, t_send, t_recv, local_sem
):
    me = lax.axis_index("tile")
    core = lax.rem(me, 2)
    pair = me // 2
    twin = pair * 2 + 1 - core
    chunk = part.shape[0] // (2 * pairs)

    def peer(d):
        return lax.rem(pair + d, pairs) * 2 + core

    def band(c, d):
        where = c * pairs + lax.rem(pair + d, pairs)
        return pl.ds(pl.multiple_of(where * chunk, chunk), chunk)

    barrier = pltpu.get_barrier_semaphore()
    for d in range(1, pairs):
        pl.semaphore_signal(barrier, inc=1, device_id={"tile": peer(d)}, device_id_type=MESH)
    pl.semaphore_signal(barrier, inc=1, device_id={"tile": twin}, device_id_type=MESH)
    pl.semaphore_wait(barrier, pairs)

    order = list(range(1, pairs)) + [0]
    copies, lines = [], []
    for d in order:
        copy = remote(
            part.at[band(1 - core, d)], got_c.at[d], c_send.at[d], c_recv.at[d], twin
        )
        copy.start()
        copies.append(copy)
    for d, copy in zip(order, copies):
        copy.wait_recv()
        value = part[band(core, d)] + got_c[d]
        if d:
            send_line[d - 1] = value.astype(BF16)
            line = remote(
                send_line.at[d - 1], got_line.at[d - 1], l_send.at[d - 1], l_recv.at[d - 1],
                peer(d),
            )
            line.start()
            lines.append(line)
        else:
            total = value
    for d in range(1, pairs):
        lines[d - 1].wait_recv()
        total += got_line[d - 1].astype(F32)
    count = own.shape[0]
    width = part.shape[1]
    for b in range(count):
        start = pl.multiple_of(me * (count * width) + b * width, width)
        factor = weight[:, pl.ds(start, width)]
        own[b] = halves(total[b * 8 : (b + 1) * 8] * factor).astype(BF16)
    sent = []

    def go(src, slot, send, recv, target):
        copy = remote(src, out.at[slot], send, recv, target)
        copy.start()
        sent.append(copy)

    for d in range(1, pairs):
        go(own, me, a_send.at[d - 1], a_recv.at[d - 1], peer(d))
    go(own, me, t_send.at[0], t_recv.at[0], twin)
    mine = pltpu.make_async_copy(own, out.at[me], local_sem)
    mine.start()
    for d in range(1, pairs):
        slot = peer(pairs - d)
        remote(own, out.at[slot], a_send.at[d - 1], a_recv.at[d - 1], slot).wait_recv()
        go(out.at[slot], slot, t_send.at[d], t_recv.at[d], twin)
    for d in range(pairs):
        slot = lax.rem(pair + pairs - d, pairs) * 2 + 1 - core
        remote(own, out.at[slot], t_send.at[d], t_recv.at[d], twin).wait_recv()
    mine.wait()
    for copy in copies + lines + sent:
        copy.wait_send()


def back_kernel(
    lines, units, contrast, level, label, part, out,
    got_c, send_y, got_y, send_z, got_z,
    c_send, c_recv, y_send, y_recv, z_send, z_recv
):
    _, core, side, step = place(lines)
    across = index_of(step, 1 - side, core)
    twin = index_of(step, side, 1 - core)
    enter(lines, step, side, core)
    chunk = part.shape[0] // (4 * lines)

    def band(c, y, z):
        return pl.ds(pl.multiple_of(((c * 2 + y) * lines + z) * chunk, chunk), chunk)

    def target(k):
        return lax.rem(step + k + 1, lines)

    c_copies = [[None] * lines, [None] * lines]
    for k in range(lines):
        for far in range(2):
            y = 1 - side if far == 0 else side
            copy = remote(
                part.at[band(1 - core, y, target(k))],
                got_c.at[far, k],
                c_send.at[far, k],
                c_recv.at[far, k],
                twin,
            )
            copy.start()
            c_copies[far][k] = copy
    y_copies = []
    for k in range(lines):
        c_copies[0][k].wait_recv()
        send_y[k] = (
            part[band(core, 1 - side, target(k))].astype(F32) + got_c[0, k].astype(F32)
        ).astype(BF16)
        copy = remote(send_y.at[k], got_y.at[k], y_send.at[k], y_recv.at[k], across)
        copy.start()
        y_copies.append(copy)
    z_copies = []
    total = None
    for k in range(lines):
        c_copies[1][k].wait_recv()
        y_copies[k].wait_recv()
        value = (
            part[band(core, side, target(k))].astype(F32)
            + got_c[1, k].astype(F32)
            + got_y[k].astype(F32)
        )
        if k < lines - 1:
            send_z[k] = value.astype(BF16)
            copy = remote(
                send_z.at[k], got_z.at[k], z_send.at[k], z_recv.at[k],
                index_of(target(k), side, core),
            )
            copy.start()
            z_copies.append(copy)
        else:
            total = value
    for copy in z_copies:
        copy.wait_recv()
    width = part.shape[1]
    for b in range(chunk // 8):
        rows = slice(b * 8, (b + 1) * 8)
        cut = pl.ds(b * width, width)
        piece = total[rows]
        for k in range(lines - 1):
            piece += got_z[k, b * 8 : (b + 1) * 8].astype(F32)
        out[:, cut] = piece * cell_scaling(level[:, cut], label[:, cut], contrast, units)
    for copy in c_copies[0] + c_copies[1] + y_copies + z_copies:
        copy.wait_send()


def params(number):
    return pltpu.CompilerParams(
        collective_id=number, has_side_effects=True, vmem_limit_bytes=VMEM_LIMIT
    )


VM = pl.BlockSpec(memory_space=pltpu.VMEM)
SM = pl.BlockSpec(memory_space=pltpu.SMEM)
ANY = pl.BlockSpec(memory_space=pl.ANY)


def shards(
    probes,
    level_set,
    unit_label,
    contrast,
    station_weight,
    u_factor,
    v_factor,
    col_owner,
    col_local,
    row_owner,
    row_local,
    tile_rank,
):
    peers = lax.axis_size("tile")
    lines = peers // 4
    own_index = lax.axis_index("tile")
    tiles, rank_max, width = u_factor.shape
    cell_total = probes.shape[1]
    cell_blocks = cell_total // width
    station_blocks = station_weight.shape[0] // (peers * width)
    units = contrast.shape[0]
    half = width // 2
    dma = pltpu.SemaphoreType.DMA

    def own_part(table):
        return lax.dynamic_slice_in_dim(table.reshape(-1), own_index * tiles, tiles)

    def places(owner, local, blocks, by_side):
        owner, local = own_part(owner), own_part(local)
        if by_side:
            moved = (owner % 2 * 2 + owner // 2 % 2) * lines + owner // 4
        else:
            moved = owner % 2 * (peers // 2) + owner // 2
        return owner * blocks + local, moved * blocks + local

    col_take, col_put = places(col_owner, col_local, cell_blocks, True)
    row_take, row_put = places(row_owner, row_local, station_blocks, False)
    ranks = own_part(tile_rank)
    u_rows = u_factor.reshape(tiles * rank_max, width)
    v_rows = v_factor.reshape(tiles * rank_max, width)
    level = level_set.reshape(1, cell_total)
    label = unit_label.reshape(1, cell_total)
    weight = station_weight.reshape(1, -1)

    with jax.named_scope("gather_cells"):
        cells = pl.pallas_call(
            functools.partial(cells_kernel, lines, units),
            out_shape=jax.ShapeDtypeStruct((peers, cell_blocks, 16, half), BF16),
            in_specs=[SM, VM, VM, VM],
            out_specs=ANY,
            scratch_shapes=[pltpu.VMEM((cell_blocks, 16, half), BF16), dma]
            + gather_sems(lines),
            compiler_params=params(0),
        )(contrast, probes, level, label)

    with jax.named_scope("forward_tiles"):
        partial = apply_tiles(
            col_take, row_put, ranks, cells.reshape(-1, 16, half), v_rows, u_rows,
            peers * station_blocks, F32, rank_max,
        )

    chunk = station_blocks * 8
    pairs = peers // 2
    with jax.named_scope("sum_stations"):
        data = pl.pallas_call(
            functools.partial(stations_kernel, pairs),
            out_shape=jax.ShapeDtypeStruct((peers, station_blocks, 16, half), BF16),
            in_specs=[VM, VM],
            out_specs=ANY,
            scratch_shapes=[
                pltpu.VMEM((pairs, chunk, width), F32),
                pltpu.VMEM((pairs - 1, chunk, width), BF16),
                pltpu.VMEM((pairs - 1, chunk, width), BF16),
                pltpu.VMEM((station_blocks, 16, half), BF16),
                dma((pairs,)),
                dma((pairs,)),
                dma((pairs - 1,)),
                dma((pairs - 1,)),
                dma((pairs - 1,)),
                dma((pairs - 1,)),
                dma((pairs,)),
                dma((pairs,)),
                dma,
            ],
            compiler_params=params(1),
        )(weight, partial)

    with jax.named_scope("adjoint_tiles"):
        spread = apply_tiles(
            row_take, col_put, ranks, data.reshape(-1, 16, half), u_rows, v_rows,
            peers * cell_blocks, BF16, rank_max,
        )

    chunk = cell_blocks * 8
    with jax.named_scope("sum_cells"):
        return pl.pallas_call(
            functools.partial(back_kernel, lines, units),
            out_shape=jax.ShapeDtypeStruct(probes.shape, F32),
            in_specs=[SM, VM, VM, VM],
            out_specs=VM,
            scratch_shapes=[
                pltpu.VMEM((2, lines, chunk, width), BF16),
                pltpu.VMEM((lines, chunk, width), BF16),
                pltpu.VMEM((lines, chunk, width), BF16),
                pltpu.VMEM((lines - 1, chunk, width), BF16),
                pltpu.VMEM((lines - 1, chunk, width), BF16),
                dma((2, lines)),
                dma((2, lines)),
                dma((lines,)),
                dma((lines,)),
                dma((lines - 1,)),
                dma((lines - 1,)),
            ],
            compiler_params=params(2),
        )(contrast, level, label, spread)


def solution(mesh):
    placed = (
        P(None, ("groups", "tile")),
        P(("groups", "tile")),
        P(("groups", "tile")),
        P("groups"),
        P("groups"),
        P(("groups", "tile"), None, None),
        P(("groups", "tile"), None, None),
        P("groups", None),
        P("groups"),
        P("groups", None),
        P("groups"),
        P("groups"),
    )
    return jax.shard_map(
        shards, mesh=mesh, in_specs=placed, out_specs=P(None, ("groups", "tile")), check_vma=False
    )
```

```python
import functools

import jax
import jax.numpy as jnp
from jax import lax
from jax.experimental import pallas as pl
from jax.experimental.pallas import tpu as pltpu
from jax.sharding import PartitionSpec as P

MESH = pl.DeviceIdType.MESH
VMEM_LIMIT = 56 * 1024 * 1024
GROUP = 8
F32 = jnp.float32
BF16 = jnp.bfloat16


def place(lines):
    me = lax.axis_index("tile")
    core = lax.rem(me, 2)
    side = lax.rem(me // 2, 2)
    step = me // 4
    return me, core, side, step


def index_of(step, side, core):
    return (step * 2 + side) * 2 + core


def enter(lines, step, side, core):
    barrier = pltpu.get_barrier_semaphore()
    for d in range(1, lines):
        peer = index_of(lax.rem(step + d, lines), side, core)
        pl.semaphore_signal(barrier, inc=1, device_id={"tile": peer}, device_id_type=MESH)
    for peer in (index_of(step, 1 - side, core), index_of(step, side, 1 - core)):
        pl.semaphore_signal(barrier, inc=1, device_id={"tile": peer}, device_id_type=MESH)
    pl.semaphore_wait(barrier, lines + 1)


def remote(src, dst, send, recv, peer):
    return pltpu.make_async_remote_copy(
        src_ref=src,
        dst_ref=dst,
        send_sem=send,
        recv_sem=recv,
        device_id={"tile": peer},
        device_id_type=MESH,
    )


def gather_shards(lines, parts, fill, own, out, local_sem, sems, step, side, core):
    send_z, recv_z, send_y, recv_y, send_c, recv_c = sems
    me = index_of(step, side, core)
    across = index_of(step, 1 - side, core)
    twin = index_of(step, side, 1 - core)
    size = own.shape[0] // parts
    started = []

    def at(slot, p):
        return out.at[slot, pl.ds(p * size, size)]

    def go(src, slot, p, send, recv, peer):
        copy = remote(src, at(slot, p), send, recv, peer)
        copy.start()
        started.append(copy)

    def arrived(slot, p, recv, peer):
        remote(at(slot, p), at(slot, p), recv, recv, peer).wait_recv()

    for p in range(parts):
        fill(p)
        piece = own.at[pl.ds(p * size, size)]
        go(piece, me, p, send_y.at[0, p], recv_y.at[0, p], across)
        for d in range(1, lines):
            peer = index_of(lax.rem(step + d, lines), side, core)
            go(piece, me, p, send_z.at[d - 1, p], recv_z.at[d - 1, p], peer)
    for p in range(parts):
        piece = own.at[pl.ds(p * size, size)]
        go(piece, me, p, send_c.at[0, p], recv_c.at[0, p], twin)
    mine = pltpu.make_async_copy(own, out.at[me], local_sem)
    mine.start()

    for p in range(parts + 1):
        if p < parts:
            for k in range(1, lines):
                slot = index_of(lax.rem(step + lines - k, lines), side, core)
                arrived(slot, p, recv_z.at[k - 1, p], me)
                go(at(slot, p), slot, p, send_y.at[k, p], recv_y.at[k, p], across)
                go(at(slot, p), slot, p, send_c.at[k, p], recv_c.at[k, p], twin)
        if p >= 1:
            for k in range(lines):
                slot = index_of(lax.rem(step + lines - k, lines), 1 - side, core)
                arrived(slot, p - 1, recv_y.at[k, p - 1], across)
                far = lines + k
                go(
                    at(slot, p - 1), slot, p - 1,
                    send_c.at[far, p - 1], recv_c.at[far, p - 1], twin,
                )
    for p in range(parts):
        for k in range(lines):
            for far in range(2):
                where = 1 - side if far else side
                slot = index_of(lax.rem(step + lines - k, lines), where, 1 - core)
                arrived(slot, p, recv_c.at[far * lines + k, p], twin)
    mine.wait()
    for copy in started:
        copy.wait_send()


def gather_sems(lines, parts):
    dma = pltpu.SemaphoreType.DMA
    return [
        dma((lines - 1, parts)),
        dma((lines - 1, parts)),
        dma((lines, parts)),
        dma((lines, parts)),
        dma((2 * lines, parts)),
        dma((2 * lines, parts)),
    ]


def cell_scaling(level, label, contrast, units):
    picked = jnp.full(level.shape, contrast[0], F32)
    for unit in range(1, units):
        picked = jnp.where(label == unit, contrast[unit], picked)
    return picked / (1.0 + level * level)


def halves(block):
    half = block.shape[1] // 2
    return jnp.concatenate([block[:, :half], block[:, half:]], axis=0)


def cells_kernel(
    lines, units, parts, contrast, probes, level, label, out, own, local_sem, *sems
):
    _, core, side, step = place(lines)
    count = own.shape[0]
    width = probes.shape[1] // count
    size = count // parts

    def fill(p):
        for b in range(p * size, (p + 1) * size):
            cut = pl.ds(b * width, width)
            scaling = cell_scaling(level[:, cut], label[:, cut], contrast, units)
            own[b] = halves(probes[:, cut] * scaling).astype(BF16)

    enter(lines, step, side, core)
    gather_shards(lines, parts, fill, own, out, local_sem, sems, step, side, core)


def tiles_kernel(
    per_step, rank_max, take, put, ranks, held, first, second, out, total
):
    i = pl.program_id(0)

    @pl.when(i == 0)
    def _():
        total[...] = jnp.zeros_like(total)

    rows = GROUP * rank_max
    lane = lax.broadcasted_iota(jnp.int32, (8, rows), 1)
    groups = range(per_step // GROUP)
    inners = []
    for g in groups:
        pieces = []
        for j in range(GROUP):
            block = held[take[i * per_step + g * GROUP + j]].astype(F32)
            pieces.append(jnp.concatenate([block[:8], block[8:]], axis=1))
        data = jnp.concatenate(pieces, axis=0).astype(BF16)
        inners.append(
            lax.dot_general(
                data,
                first[g * rows : (g + 1) * rows],
                (((1,), (1,)), ((), ())),
                preferred_element_type=F32,
            )
        )
    results = []
    for g in groups:
        kept = []
        for j in range(GROUP):
            start = j * rank_max
            end = start + ranks[i * per_step + g * GROUP + j]
            part = inners[g][j * 8 : (j + 1) * 8]
            kept.append(jnp.where((lane >= start) & (lane < end), part, 0.0))
        coeff = jnp.concatenate(kept, axis=0).astype(BF16)
        results.append(
            jnp.dot(coeff, second[g * rows : (g + 1) * rows], preferred_element_type=F32)
        )
    for g in groups:
        for j in range(GROUP):
            spot = put[i * per_step + g * GROUP + j]
            total[spot] += results[g][j * 8 : (j + 1) * 8]

    @pl.when(i == pl.num_programs(0) - 1)
    def _():
        out[...] = total[...].reshape(out.shape).astype(out.dtype)


def apply_tiles(take, put, ranks, held, first, second, blocks, dtype, rank_max):
    tiles = take.shape[0]
    per_step = 4 * GROUP
    width = second.shape[1]
    rows = per_step * rank_max
    spec = pl.BlockSpec((rows, width), lambda i, *_: (i, 0))
    return pl.pallas_call(
        functools.partial(tiles_kernel, per_step, rank_max),
        out_shape=jax.ShapeDtypeStruct((blocks * 8, width), dtype),
        grid_spec=pltpu.PrefetchScalarGridSpec(
            num_scalar_prefetch=3,
            grid=(tiles // per_step,),
            in_specs=[
                pl.BlockSpec(held.shape, lambda i, *_: (0, 0, 0)),
                spec,
                spec,
            ],
            out_specs=pl.BlockSpec((blocks * 8, width), lambda i, *_: (0, 0)),
            scratch_shapes=[pltpu.VMEM((blocks, 8, width), F32)],
        ),
        compiler_params=pltpu.CompilerParams(vmem_limit_bytes=VMEM_LIMIT),
        cost_estimate=pl.CostEstimate(
            flops=4 * tiles * GROUP * 8 * rank_max * width,
            bytes_accessed=4 * tiles * rank_max * width,
            transcendentals=0,
        ),
    )(take, put, ranks, held, first, second)


def stations_kernel(
    pairs, weight, part, out,
    got_c, send_line, got_line, own,
    c_send, c_recv, l_send, l_recv, a_send, a_recv, t_send, t_recv, local_sem
):
    me = lax.axis_index("tile")
    core = lax.rem(me, 2)
    pair = me // 2
    twin = pair * 2 + 1 - core
    chunk = part.shape[0] // (2 * pairs)

    def peer(d):
        return lax.rem(pair + d, pairs) * 2 + core

    def band(c, d):
        where = c * pairs + lax.rem(pair + d, pairs)
        return pl.ds(pl.multiple_of(where * chunk, chunk), chunk)

    barrier = pltpu.get_barrier_semaphore()
    for d in range(1, pairs):
        pl.semaphore_signal(barrier, inc=1, device_id={"tile": peer(d)}, device_id_type=MESH)
    pl.semaphore_signal(barrier, inc=1, device_id={"tile": twin}, device_id_type=MESH)
    pl.semaphore_wait(barrier, pairs)

    order = list(range(1, pairs)) + [0]
    copies, lines = [], []
    for d in order:
        copy = remote(
            part.at[band(1 - core, d)], got_c.at[d], c_send.at[d], c_recv.at[d], twin
        )
        copy.start()
        copies.append(copy)
    for d, copy in zip(order, copies):
        copy.wait_recv()
        value = part[band(core, d)] + got_c[d]
        if d:
            send_line[d - 1] = value.astype(BF16)
            line = remote(
                send_line.at[d - 1], got_line.at[d - 1], l_send.at[d - 1], l_recv.at[d - 1],
                peer(d),
            )
            line.start()
            lines.append(line)
        else:
            total = value
    for d in range(1, pairs):
        lines[d - 1].wait_recv()
        total += got_line[d - 1].astype(F32)
    count = own.shape[0]
    width = part.shape[1]
    for b in range(count):
        start = pl.multiple_of(me * (count * width) + b * width, width)
        factor = weight[:, pl.ds(start, width)]
        own[b] = halves(total[b * 8 : (b + 1) * 8] * factor).astype(BF16)
    sent = []

    def go(src, slot, send, recv, target):
        copy = remote(src, out.at[slot], send, recv, target)
        copy.start()
        sent.append(copy)

    for d in range(1, pairs):
        go(own, me, a_send.at[d - 1], a_recv.at[d - 1], peer(d))
    go(own, me, t_send.at[0], t_recv.at[0], twin)
    mine = pltpu.make_async_copy(own, out.at[me], local_sem)
    mine.start()
    for d in range(1, pairs):
        slot = peer(pairs - d)
        remote(own, out.at[slot], a_send.at[d - 1], a_recv.at[d - 1], slot).wait_recv()
        go(out.at[slot], slot, t_send.at[d], t_recv.at[d], twin)
    for d in range(pairs):
        slot = lax.rem(pair + pairs - d, pairs) * 2 + 1 - core
        remote(own, out.at[slot], t_send.at[d], t_recv.at[d], twin).wait_recv()
    mine.wait()
    for copy in copies + lines + sent:
        copy.wait_send()


def back_kernel(
    lines, units, contrast, level, label, part, out,
    got_c, send_y, got_y, send_z, got_z,
    c_send, c_recv, y_send, y_recv, z_send, z_recv
):
    _, core, side, step = place(lines)
    across = index_of(step, 1 - side, core)
    twin = index_of(step, side, 1 - core)
    enter(lines, step, side, core)
    chunk = part.shape[0] // (4 * lines)

    def band(c, y, z):
        return pl.ds(pl.multiple_of(((c * 2 + y) * lines + z) * chunk, chunk), chunk)

    def target(k):
        return lax.rem(step + k + 1, lines)

    c_copies = [[None] * lines, [None] * lines]
    for k in range(lines):
        for far in range(2):
            y = 1 - side if far == 0 else side
            copy = remote(
                part.at[band(1 - core, y, target(k))],
                got_c.at[far, k],
                c_send.at[far, k],
                c_recv.at[far, k],
                twin,
            )
            copy.start()
            c_copies[far][k] = copy
    y_copies = []
    for k in range(lines):
        c_copies[0][k].wait_recv()
        send_y[k] = (
            part[band(core, 1 - side, target(k))].astype(F32) + got_c[0, k].astype(F32)
        ).astype(BF16)
        copy = remote(send_y.at[k], got_y.at[k], y_send.at[k], y_recv.at[k], across)
        copy.start()
        y_copies.append(copy)
    z_copies = []
    total = None
    for k in range(lines):
        c_copies[1][k].wait_recv()
        y_copies[k].wait_recv()
        value = (
            part[band(core, side, target(k))].astype(F32)
            + got_c[1, k].astype(F32)
            + got_y[k].astype(F32)
        )
        if k < lines - 1:
            send_z[k] = value.astype(BF16)
            copy = remote(
                send_z.at[k], got_z.at[k], z_send.at[k], z_recv.at[k],
                index_of(target(k), side, core),
            )
            copy.start()
            z_copies.append(copy)
        else:
            total = value
    for copy in z_copies:
        copy.wait_recv()
    width = part.shape[1]
    for b in range(chunk // 8):
        rows = slice(b * 8, (b + 1) * 8)
        cut = pl.ds(b * width, width)
        piece = total[rows]
        for k in range(lines - 1):
            piece += got_z[k, b * 8 : (b + 1) * 8].astype(F32)
        out[:, cut] = piece * cell_scaling(level[:, cut], label[:, cut], contrast, units)
    for copy in c_copies[0] + c_copies[1] + y_copies + z_copies:
        copy.wait_send()


def params(number):
    return pltpu.CompilerParams(
        collective_id=number, has_side_effects=True, vmem_limit_bytes=VMEM_LIMIT
    )


VM = pl.BlockSpec(memory_space=pltpu.VMEM)
SM = pl.BlockSpec(memory_space=pltpu.SMEM)
ANY = pl.BlockSpec(memory_space=pl.ANY)


def shards(
    probes,
    level_set,
    unit_label,
    contrast,
    station_weight,
    u_factor,
    v_factor,
    col_owner,
    col_local,
    row_owner,
    row_local,
    tile_rank,
):
    peers = lax.axis_size("tile")
    lines = peers // 4
    own_index = lax.axis_index("tile")
    tiles, rank_max, width = u_factor.shape
    cell_total = probes.shape[1]
    cell_blocks = cell_total // width
    station_blocks = station_weight.shape[0] // (peers * width)
    units = contrast.shape[0]
    half = width // 2
    parts = 4 if cell_blocks % 4 == 0 else 1
    dma = pltpu.SemaphoreType.DMA

    def own_part(table):
        return lax.dynamic_slice_in_dim(table.reshape(-1), own_index * tiles, tiles)

    def places(owner, local, blocks, by_side):
        owner, local = own_part(owner), own_part(local)
        if by_side:
            moved = (owner % 2 * 2 + owner // 2 % 2) * lines + owner // 4
        else:
            moved = owner % 2 * (peers // 2) + owner // 2
        return owner * blocks + local, moved * blocks + local

    col_take, col_put = places(col_owner, col_local, cell_blocks, True)
    row_take, row_put = places(row_owner, row_local, station_blocks, False)
    ranks = own_part(tile_rank)
    u_rows = u_factor.reshape(tiles * rank_max, width)
    v_rows = v_factor.reshape(tiles * rank_max, width)
    level = level_set.reshape(1, cell_total)
    label = unit_label.reshape(1, cell_total)
    weight = station_weight.reshape(1, -1)

    with jax.named_scope("gather_cells"):
        cells = pl.pallas_call(
            functools.partial(cells_kernel, lines, units, parts),
            out_shape=jax.ShapeDtypeStruct((peers, cell_blocks, 16, half), BF16),
            in_specs=[SM, VM, VM, VM],
            out_specs=ANY,
            scratch_shapes=[pltpu.VMEM((cell_blocks, 16, half), BF16), dma]
            + gather_sems(lines, parts),
            compiler_params=params(0),
        )(contrast, probes, level, label)

    with jax.named_scope("forward_tiles"):
        partial = apply_tiles(
            col_take, row_put, ranks, cells.reshape(-1, 16, half), v_rows, u_rows,
            peers * station_blocks, F32, rank_max,
        )

    chunk = station_blocks * 8
    pairs = peers // 2
    with jax.named_scope("sum_stations"):
        data = pl.pallas_call(
            functools.partial(stations_kernel, pairs),
            out_shape=jax.ShapeDtypeStruct((peers, station_blocks, 16, half), BF16),
            in_specs=[VM, VM],
            out_specs=ANY,
            scratch_shapes=[
                pltpu.VMEM((pairs, chunk, width), F32),
                pltpu.VMEM((pairs - 1, chunk, width), BF16),
                pltpu.VMEM((pairs - 1, chunk, width), BF16),
                pltpu.VMEM((station_blocks, 16, half), BF16),
                dma((pairs,)),
                dma((pairs,)),
                dma((pairs - 1,)),
                dma((pairs - 1,)),
                dma((pairs - 1,)),
                dma((pairs - 1,)),
                dma((pairs,)),
                dma((pairs,)),
                dma,
            ],
            compiler_params=params(1),
        )(weight, partial)

    with jax.named_scope("adjoint_tiles"):
        spread = apply_tiles(
            row_take, col_put, ranks, data.reshape(-1, 16, half), u_rows, v_rows,
            peers * cell_blocks, BF16, rank_max,
        )

    chunk = cell_blocks * 8
    with jax.named_scope("sum_cells"):
        return pl.pallas_call(
            functools.partial(back_kernel, lines, units),
            out_shape=jax.ShapeDtypeStruct(probes.shape, F32),
            in_specs=[SM, VM, VM, VM],
            out_specs=VM,
            scratch_shapes=[
                pltpu.VMEM((2, lines, chunk, width), BF16),
                pltpu.VMEM((lines, chunk, width), BF16),
                pltpu.VMEM((lines, chunk, width), BF16),
                pltpu.VMEM((lines - 1, chunk, width), BF16),
                pltpu.VMEM((lines - 1, chunk, width), BF16),
                dma((2, lines)),
                dma((2, lines)),
                dma((lines,)),
                dma((lines,)),
                dma((lines - 1,)),
                dma((lines - 1,)),
            ],
            compiler_params=params(2),
        )(contrast, level, label, spread)


def solution(mesh):
    placed = (
        P(None, ("groups", "tile")),
        P(("groups", "tile")),
        P(("groups", "tile")),
        P("groups"),
        P("groups"),
        P(("groups", "tile"), None, None),
        P(("groups", "tile"), None, None),
        P("groups", None),
        P("groups"),
        P("groups", None),
        P("groups"),
        P("groups"),
    )
    return jax.shard_map(
        shards, mesh=mesh, in_specs=placed, out_specs=P(None, ("groups", "tile")), check_vma=False
    )
```

```python
import functools

import jax
import jax.numpy as jnp
from jax import lax
from jax.experimental import pallas as pl
from jax.experimental.pallas import tpu as pltpu
from jax.sharding import PartitionSpec as P

MESH = pl.DeviceIdType.MESH
VMEM_LIMIT = 56 * 1024 * 1024
GROUP = 8
F32 = jnp.float32
BF16 = jnp.bfloat16


def place(lines):
    me = lax.axis_index("tile")
    core = lax.rem(me, 2)
    side = lax.rem(me // 2, 2)
    step = me // 4
    return me, core, side, step


def index_of(step, side, core):
    return (step * 2 + side) * 2 + core


def enter(lines, step, side, core):
    barrier = pltpu.get_barrier_semaphore()
    for d in range(1, lines):
        peer = index_of(lax.rem(step + d, lines), side, core)
        pl.semaphore_signal(barrier, inc=1, device_id={"tile": peer}, device_id_type=MESH)
    for peer in (index_of(step, 1 - side, core), index_of(step, side, 1 - core)):
        pl.semaphore_signal(barrier, inc=1, device_id={"tile": peer}, device_id_type=MESH)
    pl.semaphore_wait(barrier, lines + 1)


def remote(src, dst, send, recv, peer):
    return pltpu.make_async_remote_copy(
        src_ref=src,
        dst_ref=dst,
        send_sem=send,
        recv_sem=recv,
        device_id={"tile": peer},
        device_id_type=MESH,
    )


def gather_shards(lines, parts, fill, own, out, local_sem, sems, step, side, core):
    send_z, recv_z, send_y, recv_y, send_c, recv_c = sems
    me = index_of(step, side, core)
    across = index_of(step, 1 - side, core)
    twin = index_of(step, side, 1 - core)
    size = own.shape[0] // parts
    started = []

    def at(slot, p):
        return out.at[slot, pl.ds(p * size, size)]

    def go(src, slot, p, send, recv, peer):
        copy = remote(src, at(slot, p), send, recv, peer)
        copy.start()
        started.append(copy)

    def arrived(slot, p, recv, peer):
        remote(at(slot, p), at(slot, p), recv, recv, peer).wait_recv()

    for p in range(parts):
        fill(p)
        piece = own.at[pl.ds(p * size, size)]
        go(piece, me, p, send_y.at[0, p], recv_y.at[0, p], across)
        for d in range(1, lines):
            peer = index_of(lax.rem(step + d, lines), side, core)
            go(piece, me, p, send_z.at[d - 1, p], recv_z.at[d - 1, p], peer)
    for p in range(parts):
        piece = own.at[pl.ds(p * size, size)]
        go(piece, me, p, send_c.at[0, p], recv_c.at[0, p], twin)
    mine = pltpu.make_async_copy(own, out.at[me], local_sem)
    mine.start()

    for p in range(parts + 1):
        if p < parts:
            for k in range(1, lines):
                slot = index_of(lax.rem(step + lines - k, lines), side, core)
                arrived(slot, p, recv_z.at[k - 1, p], me)
                go(at(slot, p), slot, p, send_y.at[k, p], recv_y.at[k, p], across)
                go(at(slot, p), slot, p, send_c.at[k, p], recv_c.at[k, p], twin)
        if p >= 1:
            for k in range(lines):
                slot = index_of(lax.rem(step + lines - k, lines), 1 - side, core)
                arrived(slot, p - 1, recv_y.at[k, p - 1], across)
                far = lines + k
                go(
                    at(slot, p - 1), slot, p - 1,
                    send_c.at[far, p - 1], recv_c.at[far, p - 1], twin,
                )
    for p in range(parts):
        for k in range(lines):
            for far in range(2):
                where = 1 - side if far else side
                slot = index_of(lax.rem(step + lines - k, lines), where, 1 - core)
                arrived(slot, p, recv_c.at[far * lines + k, p], twin)
    mine.wait()
    for copy in started:
        copy.wait_send()


def gather_sems(lines, parts):
    dma = pltpu.SemaphoreType.DMA
    return [
        dma((lines - 1, parts)),
        dma((lines - 1, parts)),
        dma((lines, parts)),
        dma((lines, parts)),
        dma((2 * lines, parts)),
        dma((2 * lines, parts)),
    ]


def cell_scaling(level, label, contrast, units):
    picked = jnp.full(level.shape, contrast[0], F32)
    for unit in range(1, units):
        picked = jnp.where(label == unit, contrast[unit], picked)
    return picked / (1.0 + level * level)


def halves(block):
    half = block.shape[1] // 2
    return jnp.concatenate([block[:, :half], block[:, half:]], axis=0)


def cells_kernel(
    lines, units, parts, contrast, probes, level, label, out, own, local_sem, *sems
):
    _, core, side, step = place(lines)
    count = own.shape[0]
    width = probes.shape[1] // count
    size = count // parts

    def fill(p):
        for b in range(p * size, (p + 1) * size):
            cut = pl.ds(b * width, width)
            scaling = cell_scaling(level[:, cut], label[:, cut], contrast, units)
            own[b] = halves(probes[:, cut] * scaling).astype(BF16)

    enter(lines, step, side, core)
    gather_shards(lines, parts, fill, own, out, local_sem, sems, step, side, core)


def tiles_kernel(
    per_step, rank_max, take, put, ranks, held, first, second, out, total
):
    i = pl.program_id(0)

    @pl.when(i == 0)
    def _():
        total[...] = jnp.zeros_like(total)

    rows = GROUP * rank_max
    lane = lax.broadcasted_iota(jnp.int32, (8, rows), 1)
    groups = range(per_step // GROUP)
    inners = []
    for g in groups:
        pieces = []
        for j in range(GROUP):
            block = held[take[i * per_step + g * GROUP + j]].astype(F32)
            pieces.append(jnp.concatenate([block[:8], block[8:]], axis=1))
        data = jnp.concatenate(pieces, axis=0).astype(BF16)
        inners.append(
            lax.dot_general(
                data,
                first[g * rows : (g + 1) * rows],
                (((1,), (1,)), ((), ())),
                preferred_element_type=F32,
            )
        )
    results = []
    for g in groups:
        kept = []
        for j in range(GROUP):
            start = j * rank_max
            end = start + ranks[i * per_step + g * GROUP + j]
            part = inners[g][j * 8 : (j + 1) * 8]
            kept.append(jnp.where((lane >= start) & (lane < end), part, 0.0))
        coeff = jnp.concatenate(kept, axis=0).astype(BF16)
        results.append(
            jnp.dot(coeff, second[g * rows : (g + 1) * rows], preferred_element_type=F32)
        )
    for g in groups:
        for j in range(GROUP):
            spot = put[i * per_step + g * GROUP + j]
            total[spot] += results[g][j * 8 : (j + 1) * 8]

    @pl.when(i == pl.num_programs(0) - 1)
    def _():
        out[...] = total[...].reshape(out.shape).astype(out.dtype)


def apply_tiles(take, put, ranks, held, first, second, blocks, dtype, rank_max):
    tiles = take.shape[0]
    per_step = 4 * GROUP
    width = second.shape[1]
    rows = per_step * rank_max
    spec = pl.BlockSpec((rows, width), lambda i, *_: (i, 0))
    return pl.pallas_call(
        functools.partial(tiles_kernel, per_step, rank_max),
        out_shape=jax.ShapeDtypeStruct((blocks * 8, width), dtype),
        grid_spec=pltpu.PrefetchScalarGridSpec(
            num_scalar_prefetch=3,
            grid=(tiles // per_step,),
            in_specs=[
                pl.BlockSpec(held.shape, lambda i, *_: (0, 0, 0)),
                spec,
                spec,
            ],
            out_specs=pl.BlockSpec((blocks * 8, width), lambda i, *_: (0, 0)),
            scratch_shapes=[pltpu.VMEM((blocks, 8, width), F32)],
        ),
        compiler_params=pltpu.CompilerParams(vmem_limit_bytes=VMEM_LIMIT),
        cost_estimate=pl.CostEstimate(
            flops=4 * tiles * GROUP * 8 * rank_max * width,
            bytes_accessed=4 * tiles * rank_max * width,
            transcendentals=0,
        ),
    )(take, put, ranks, held, first, second)


def stations_phase(
    pairs, weight, part, out,
    got_c, send_line, got_line, own,
    c_send, c_recv, l_send, l_recv, a_send, a_recv, t_send, t_recv, local_sem
):
    me = lax.axis_index("tile")
    core = lax.rem(me, 2)
    pair = me // 2
    twin = pair * 2 + 1 - core
    chunk = part.shape[0] // (2 * pairs)
    count = own.shape[0]
    width = part.shape[1]

    def peer(d):
        return lax.rem(pair + d, pairs) * 2 + core

    def band(c, d):
        where = c * pairs + lax.rem(pair + d, pairs)
        return pl.ds(pl.multiple_of(where * chunk, chunk), chunk)

    def shard(slot):
        return out.at[pl.ds(slot * count, count)]

    order = list(range(1, pairs)) + [0]
    copies, lines = [], []
    for d in order:
        copy = remote(
            part.at[band(1 - core, d)], got_c.at[d], c_send.at[d], c_recv.at[d], twin
        )
        copy.start()
        copies.append(copy)
    for d, copy in zip(order, copies):
        copy.wait_recv()
        value = part[band(core, d)] + got_c[d]
        if d:
            send_line[d - 1] = value.astype(BF16)
            line = remote(
                send_line.at[d - 1], got_line.at[d - 1], l_send.at[d - 1], l_recv.at[d - 1],
                peer(d),
            )
            line.start()
            lines.append(line)
        else:
            total = value
    for d in range(1, pairs):
        lines[d - 1].wait_recv()
        total += got_line[d - 1].astype(F32)
    for b in range(count):
        start = pl.multiple_of(me * (count * width) + b * width, width)
        factor = weight[:, pl.ds(start, width)]
        own[b] = halves(total[b * 8 : (b + 1) * 8] * factor).astype(BF16)
    sent = []

    def go(src, slot, send, recv, target):
        copy = remote(src, shard(slot), send, recv, target)
        copy.start()
        sent.append(copy)

    for d in range(1, pairs):
        go(own, me, a_send.at[d - 1], a_recv.at[d - 1], peer(d))
    go(own, me, t_send.at[0], t_recv.at[0], twin)
    mine = pltpu.make_async_copy(own, shard(me), local_sem)
    mine.start()
    for d in range(1, pairs):
        slot = peer(pairs - d)
        remote(own, shard(slot), a_send.at[d - 1], a_recv.at[d - 1], slot).wait_recv()
        go(shard(slot), slot, t_send.at[d], t_recv.at[d], twin)
    for d in range(pairs):
        slot = lax.rem(pair + pairs - d, pairs) * 2 + 1 - core
        remote(own, shard(slot), t_send.at[d], t_recv.at[d], twin).wait_recv()
    mine.wait()
    return copies + lines + sent


def adjoint_kernel(
    lines, units, capacity, rank_max,
    contrast, slot_tile, slot_row, slot_rank, target_row, level, label, weight, part, u_hbm, v_hbm,
    out,
    u_here, v_here, data,
    got_c, send_line, got_line, own,
    send_twin, got_twin, send_y, got_y, near, send_z, got_z,
    c_send, c_recv, l_send, l_recv, a_send, a_recv, t_send, t_recv, local_sem, u_sem, v_sem,
    x_send, x_recv, y_send, y_recv, z_send, z_recv
):
    me, core, side, step = place(lines)
    pairs = 2 * lines
    across = index_of(step, 1 - side, core)
    twin = index_of(step, side, 1 - core)
    barrier = pltpu.get_barrier_semaphore()
    for d in range(1, pairs):
        peer = lax.rem(me // 2 + d, pairs) * 2 + core
        pl.semaphore_signal(barrier, inc=1, device_id={"tile": peer}, device_id_type=MESH)
    pl.semaphore_signal(barrier, inc=1, device_id={"tile": twin}, device_id_type=MESH)
    u_copy = pltpu.make_async_copy(u_hbm, u_here, u_sem)
    v_copy = pltpu.make_async_copy(v_hbm, v_here, v_sem)
    u_copy.start()
    v_copy.start()
    pl.semaphore_wait(barrier, pairs)
    pending = stations_phase(
        pairs, weight, part, data,
        got_c, send_line, got_line, own,
        c_send, c_recv, l_send, l_recv, a_send, a_recv, t_send, t_recv, local_sem,
    )
    u_copy.wait()
    v_copy.wait()

    size = min(GROUP, capacity)
    groups = capacity // size
    rows = size * rank_max
    chunk = near.shape[1]
    lane = lax.broadcasted_iota(jnp.int32, (8, rows), 1)
    line = lax.broadcasted_iota(jnp.int32, (chunk, size * 8), 0)

    def chunks(owners):
        jobs = [(o, g) for o in owners for g in range(groups)]
        inners = []
        for o, g in jobs:
            pieces, factors = [], []
            for j in range(size):
                s = o * capacity + g * size + j
                block = data[slot_row[s]].astype(F32)
                pieces.append(jnp.concatenate([block[:8], block[8:]], axis=1))
                factors.append(u_here[slot_tile[s]])
            inners.append(
                lax.dot_general(
                    jnp.concatenate(pieces, axis=0).astype(BF16),
                    jnp.concatenate(factors, axis=0),
                    (((1,), (1,)), ((), ())),
                    preferred_element_type=F32,
                )
            )
        spread = []
        for (o, g), inner in zip(jobs, inners):
            kept = []
            for j in range(size):
                start = j * rank_max
                end = start + slot_rank[o * capacity + g * size + j]
                piece = inner[j * 8 : (j + 1) * 8]
                kept.append(jnp.where((lane >= start) & (lane < end), piece, 0.0))
            kept = jnp.concatenate(kept, axis=0).astype(BF16)
            chosen = jnp.where(line == target_row[o * groups + g], 1.0, 0.0).astype(BF16)
            spread.append(jnp.dot(chosen, kept, preferred_element_type=F32).astype(BF16))
        values = []
        for n in range(len(owners)):
            value = None
            for g in range(groups):
                s = owners[n] * capacity + g * size
                factors = jnp.concatenate([v_here[slot_tile[s + j]] for j in range(size)], axis=0)
                term = jnp.dot(spread[n * groups + g], factors, preferred_element_type=F32)
                value = term if value is None else value + term
            values.append(value)
        return values

    def target(k):
        return lax.rem(step + k + 1, lines)

    def twin_copy(far, k):
        return remote(
            send_twin.at[far, k], got_twin.at[far, k], x_send.at[far, k], x_recv.at[far, k], twin
        )

    def y_copy(k):
        return remote(send_y.at[k], got_y.at[k], y_send.at[k], y_recv.at[k], across)

    def z_copy(k):
        return remote(
            send_z.at[k], got_z.at[k], z_send.at[k], z_recv.at[k],
            index_of(target(k), side, core),
        )

    def one_target(k, _):
        there = target(k)
        first, second = chunks(
            [index_of(there, 1 - side, 1 - core), index_of(there, side, 1 - core)]
        )
        send_twin[0, k] = first.astype(BF16)
        twin_copy(0, k).start()
        send_twin[1, k] = second.astype(BF16)
        twin_copy(1, k).start()
        first, second = chunks([index_of(there, 1 - side, core), index_of(there, side, core)])
        twin_copy(0, k).wait_recv()
        send_y[k] = (first + got_twin[0, k].astype(F32)).astype(BF16)
        y_copy(k).start()
        twin_copy(1, k).wait_recv()
        near[k] = second + got_twin[1, k].astype(F32)

        @pl.when(k > 0)
        def _():
            y_copy(k - 1).wait_recv()
            send_z[k - 1] = (near[k - 1] + got_y[k - 1].astype(F32)).astype(BF16)
            z_copy(k - 1).start()

        return 0

    lax.fori_loop(0, lines, one_target, 0)
    y_copy(lines - 1).wait_recv()
    for k in range(lines - 1):
        z_copy(k).wait_recv()
    width = part.shape[1]
    for b in range(chunk // 8):
        cut = pl.ds(b * width, width)
        band = slice(b * 8, (b + 1) * 8)
        piece = near[lines - 1, band] + got_y[lines - 1, band].astype(F32)
        for k in range(lines - 1):
            piece += got_z[k, band].astype(F32)
        out[:, cut] = piece * cell_scaling(level[:, cut], label[:, cut], contrast, units)
    for copy in pending:
        copy.wait_send()
    for k in range(lines):
        twin_copy(0, k).wait_send()
        twin_copy(1, k).wait_send()
        y_copy(k).wait_send()
        if k < lines - 1:
            z_copy(k).wait_send()


def params(number):
    return pltpu.CompilerParams(
        collective_id=number, has_side_effects=True, vmem_limit_bytes=VMEM_LIMIT
    )


VM = pl.BlockSpec(memory_space=pltpu.VMEM)
SM = pl.BlockSpec(memory_space=pltpu.SMEM)
ANY = pl.BlockSpec(memory_space=pl.ANY)


def shards(
    probes,
    level_set,
    unit_label,
    contrast,
    station_weight,
    u_factor,
    v_factor,
    col_owner,
    col_local,
    row_owner,
    row_local,
    tile_rank,
):
    peers = lax.axis_size("tile")
    lines = peers // 4
    own_index = lax.axis_index("tile")
    tiles, rank_max, width = u_factor.shape
    cell_total = probes.shape[1]
    cell_blocks = cell_total // width
    station_blocks = station_weight.shape[0] // (peers * width)
    units = contrast.shape[0]
    half = width // 2
    parts = 4 if cell_blocks % 4 == 0 else 1
    dma = pltpu.SemaphoreType.DMA

    capacity = max(2, 2 * tiles // peers)
    size = min(GROUP, capacity)

    def own_part(table):
        return lax.dynamic_slice_in_dim(table.reshape(-1), own_index * tiles, tiles)

    owner, local = own_part(col_owner), own_part(col_local)
    row_who, row_where = own_part(row_owner), own_part(row_local)
    ranks = own_part(tile_rank)
    col_take = owner * cell_blocks + local
    row_take = row_who * station_blocks + row_where
    row_put = (row_who % 2 * (peers // 2) + row_who // 2) * station_blocks + row_where

    number = jnp.arange(tiles, dtype=jnp.int32)
    earlier = (owner[None, :] == owner[:, None]) & (number[None, :] < number[:, None])
    slot = owner * capacity + jnp.sum(earlier.astype(jnp.int32), axis=1)
    rank_range = rank_max + 1
    row_range = peers * station_blocks
    packed = ((number * row_range + row_take) * rank_range + ranks) * cell_blocks + local
    held = jnp.arange(peers * capacity, dtype=jnp.int32)[:, None] == slot[None, :]
    packed = jnp.sum(jnp.where(held, packed[None, :], 0), axis=1)
    slot_local = packed % cell_blocks
    packed = packed // cell_blocks
    slot_rank = packed % rank_range
    packed = packed // rank_range
    slot_row = packed % row_range
    slot_tile = packed // row_range
    target_row = (
        slot_local[:, None] * 8 + jnp.arange(8, dtype=jnp.int32)[None, :]
    ).reshape(peers * capacity // size, 1, size * 8)

    u_rows = u_factor.reshape(tiles * rank_max, width)
    v_rows = v_factor.reshape(tiles * rank_max, width)
    level = level_set.reshape(1, cell_total)
    label = unit_label.reshape(1, cell_total)
    weight = station_weight.reshape(1, -1)

    with jax.named_scope("gather_cells"):
        cells = pl.pallas_call(
            functools.partial(cells_kernel, lines, units, parts),
            out_shape=jax.ShapeDtypeStruct((peers, cell_blocks, 16, half), BF16),
            in_specs=[SM, VM, VM, VM],
            out_specs=ANY,
            scratch_shapes=[pltpu.VMEM((cell_blocks, 16, half), BF16), dma]
            + gather_sems(lines, parts),
            compiler_params=params(0),
        )(contrast, probes, level, label)

    with jax.named_scope("forward_tiles"):
        partial = apply_tiles(
            col_take, row_put, ranks, cells.reshape(-1, 16, half), v_rows, u_rows,
            peers * station_blocks, F32, rank_max,
        )

    small = station_blocks * 8
    chunk = cell_blocks * 8
    pairs = peers // 2
    factors = pltpu.VMEM((tiles, rank_max, width), BF16)
    with jax.named_scope("stations_and_adjoint"):
        return pl.pallas_call(
            functools.partial(adjoint_kernel, lines, units, capacity, rank_max),
            out_shape=jax.ShapeDtypeStruct(probes.shape, F32),
            in_specs=[SM, SM, SM, SM, VM, VM, VM, VM, VM, ANY, ANY],
            out_specs=VM,
            scratch_shapes=[
                factors,
                factors,
                pltpu.VMEM((peers * station_blocks, 16, half), BF16),
                pltpu.VMEM((pairs, small, width), F32),
                pltpu.VMEM((pairs - 1, small, width), BF16),
                pltpu.VMEM((pairs - 1, small, width), BF16),
                pltpu.VMEM((station_blocks, 16, half), BF16),
                pltpu.VMEM((2, lines, chunk, width), BF16),
                pltpu.VMEM((2, lines, chunk, width), BF16),
                pltpu.VMEM((lines, chunk, width), BF16),
                pltpu.VMEM((lines, chunk, width), BF16),
                pltpu.VMEM((lines, chunk, width), F32),
                pltpu.VMEM((lines - 1, chunk, width), BF16),
                pltpu.VMEM((lines - 1, chunk, width), BF16),
                dma((pairs,)),
                dma((pairs,)),
                dma((pairs - 1,)),
                dma((pairs - 1,)),
                dma((pairs - 1,)),
                dma((pairs - 1,)),
                dma((pairs,)),
                dma((pairs,)),
                dma,
                dma,
                dma,
                dma((2, lines)),
                dma((2, lines)),
                dma((lines,)),
                dma((lines,)),
                dma((lines - 1,)),
                dma((lines - 1,)),
            ],
            compiler_params=params(1),
        )(
            contrast, slot_tile, slot_row, slot_rank, target_row, level, label, weight, partial,
            u_factor, v_factor,
        )


def solution(mesh):
    placed = (
        P(None, ("groups", "tile")),
        P(("groups", "tile")),
        P(("groups", "tile")),
        P("groups"),
        P("groups"),
        P(("groups", "tile"), None, None),
        P(("groups", "tile"), None, None),
        P("groups", None),
        P("groups"),
        P("groups", None),
        P("groups"),
        P("groups"),
    )
    return jax.shard_map(
        shards, mesh=mesh, in_specs=placed, out_specs=P(None, ("groups", "tile")), check_vma=False
    )
```

```python
import functools

import jax
import jax.numpy as jnp
from jax import lax
from jax.experimental import pallas as pl
from jax.experimental.pallas import tpu as pltpu
from jax.sharding import PartitionSpec as P

MESH = pl.DeviceIdType.MESH
VMEM_LIMIT = 56 * 1024 * 1024
GROUP = 8
F32 = jnp.float32
BF16 = jnp.bfloat16


def place(lines):
    me = lax.axis_index("tile")
    core = lax.rem(me, 2)
    side = lax.rem(me // 2, 2)
    step = me // 4
    return me, core, side, step


def index_of(step, side, core):
    return (step * 2 + side) * 2 + core


def remote(src, dst, send, recv, peer):
    return pltpu.make_async_remote_copy(
        src_ref=src,
        dst_ref=dst,
        send_sem=send,
        recv_sem=recv,
        device_id={"tile": peer},
        device_id_type=MESH,
    )


def gather_shards(lines, parts, fill, own, out, local_sem, sems, step, side, core):
    send_z, recv_z, send_y, recv_y, send_c, recv_c = sems
    me = index_of(step, side, core)
    across = index_of(step, 1 - side, core)
    twin = index_of(step, side, 1 - core)
    count = own.shape[0]
    size = count // parts
    started = []

    def at(slot, p):
        return out.at[pl.ds(slot * count + p * size, size)]

    def go(src, slot, p, send, recv, peer):
        copy = remote(src, at(slot, p), send, recv, peer)
        copy.start()
        started.append(copy)

    def arrived(slot, p, recv, peer):
        remote(at(slot, p), at(slot, p), recv, recv, peer).wait_recv()

    for p in range(parts):
        fill(p)
        piece = own.at[pl.ds(p * size, size)]
        go(piece, me, p, send_y.at[0, p], recv_y.at[0, p], across)
        for d in range(1, lines):
            peer = index_of(lax.rem(step + d, lines), side, core)
            go(piece, me, p, send_z.at[d - 1, p], recv_z.at[d - 1, p], peer)
    for p in range(parts):
        piece = own.at[pl.ds(p * size, size)]
        go(piece, me, p, send_c.at[0, p], recv_c.at[0, p], twin)
    mine = pltpu.make_async_copy(own, out.at[pl.ds(me * count, count)], local_sem)
    mine.start()

    for p in range(parts + 1):
        if p < parts:
            for k in range(1, lines):
                slot = index_of(lax.rem(step + lines - k, lines), side, core)
                arrived(slot, p, recv_z.at[k - 1, p], me)
                go(at(slot, p), slot, p, send_y.at[k, p], recv_y.at[k, p], across)
                go(at(slot, p), slot, p, send_c.at[k, p], recv_c.at[k, p], twin)
        if p >= 1:
            for k in range(lines):
                slot = index_of(lax.rem(step + lines - k, lines), 1 - side, core)
                arrived(slot, p - 1, recv_y.at[k, p - 1], across)
                far = lines + k
                go(
                    at(slot, p - 1), slot, p - 1,
                    send_c.at[far, p - 1], recv_c.at[far, p - 1], twin,
                )
    for p in range(parts):
        for k in range(lines):
            for far in range(2):
                where = 1 - side if far else side
                slot = index_of(lax.rem(step + lines - k, lines), where, 1 - core)
                arrived(slot, p, recv_c.at[far * lines + k, p], twin)
    mine.wait()
    return started


def gather_sems(lines, parts):
    dma = pltpu.SemaphoreType.DMA
    return [
        dma((lines - 1, parts)),
        dma((lines - 1, parts)),
        dma((lines, parts)),
        dma((lines, parts)),
        dma((2 * lines, parts)),
        dma((2 * lines, parts)),
    ]


def cell_scaling(level, label, contrast, units):
    picked = jnp.full(level.shape, contrast[0], F32)
    for unit in range(1, units):
        picked = jnp.where(label == unit, contrast[unit], picked)
    return picked / (1.0 + level * level)


def halves(block):
    half = block.shape[1] // 2
    return jnp.concatenate([block[:, :half], block[:, half:]], axis=0)


def block_chunks(owners, tables, capacity, rank_max, chunk, source, inward, outward):
    tile_of, block_of, rank_of, target_row = tables
    size = min(GROUP, capacity)
    groups = capacity // size
    rows = size * rank_max
    lane = lax.broadcasted_iota(jnp.int32, (8, rows), 1)
    line = lax.broadcasted_iota(jnp.int32, (chunk, size * 8), 0)
    jobs = [(o, g) for o in owners for g in range(groups)]
    inners = []
    for o, g in jobs:
        pieces, factors = [], []
        for j in range(size):
            s = o * capacity + g * size + j
            block = source[block_of[s]].astype(F32)
            pieces.append(jnp.concatenate([block[:8], block[8:]], axis=1))
            factors.append(inward[tile_of[s]])
        inners.append(
            lax.dot_general(
                jnp.concatenate(pieces, axis=0).astype(BF16),
                jnp.concatenate(factors, axis=0),
                (((1,), (1,)), ((), ())),
                preferred_element_type=F32,
            )
        )
    spread = []
    for (o, g), inner in zip(jobs, inners):
        kept = []
        for j in range(size):
            start = j * rank_max
            end = start + rank_of[o * capacity + g * size + j]
            piece = inner[j * 8 : (j + 1) * 8]
            kept.append(jnp.where((lane >= start) & (lane < end), piece, 0.0))
        kept = jnp.concatenate(kept, axis=0).astype(BF16)
        chosen = jnp.where(line == target_row[o * groups + g], 1.0, 0.0).astype(BF16)
        spread.append(jnp.dot(chosen, kept, preferred_element_type=F32).astype(BF16))
    values = []
    for n in range(len(owners)):
        value = None
        for g in range(groups):
            s = owners[n] * capacity + g * size
            factors = jnp.concatenate([outward[tile_of[s + j]] for j in range(size)], axis=0)
            term = jnp.dot(spread[n * groups + g], factors, preferred_element_type=F32)
            value = term if value is None else value + term
        values.append(value)
    return values


def stations_phase(
    pairs, chunks, weight, out,
    part, near, got_c, send_line, got_line, own,
    c_send, c_recv, l_send, l_recv, a_send, a_recv, t_send, t_recv, local_sem
):
    me = lax.axis_index("tile")
    core = lax.rem(me, 2)
    pair = me // 2
    twin = pair * 2 + 1 - core
    count = own.shape[0]
    width = part.shape[2]

    def peer(d):
        return lax.rem(pair + d, pairs) * 2 + core

    def shard(slot):
        return out.at[pl.ds(slot * count, count)]

    def c_copy(i):
        return remote(part.at[i], got_c.at[i], c_send.at[i], c_recv.at[i], twin)

    def line(i):
        return remote(
            send_line.at[i], got_line.at[i], l_send.at[i], l_recv.at[i], peer(i + 1)
        )

    def one_pair(i, _):
        there = lax.rem(pair + i + 1, pairs) * 2
        first, second = chunks([there + 1 - core, there + core])
        part[i] = first
        c_copy(i).start()
        near[i] = second

        @pl.when(i > 0)
        def _():
            c_copy(i - 1).wait_recv()
            send_line[i - 1] = (near[i - 1] + got_c[i - 1]).astype(BF16)
            line(i - 1).start()

        return 0

    lax.fori_loop(0, pairs, one_pair, 0)
    c_copy(pairs - 1).wait_recv()
    total = near[pairs - 1] + got_c[pairs - 1]
    copies = [c_copy(i) for i in range(pairs)]
    lines = [line(i) for i in range(pairs - 1)]
    for i in range(pairs - 1):
        lines[i].wait_recv()
        total += got_line[i].astype(F32)
    for b in range(count):
        start = pl.multiple_of(me * (count * width) + b * width, width)
        factor = weight[:, pl.ds(start, width)]
        own[b] = halves(total[b * 8 : (b + 1) * 8] * factor).astype(BF16)
    sent = []

    def go(src, slot, send, recv, target):
        copy = remote(src, shard(slot), send, recv, target)
        copy.start()
        sent.append(copy)

    for d in range(1, pairs):
        go(own, me, a_send.at[d - 1], a_recv.at[d - 1], peer(d))
    go(own, me, t_send.at[0], t_recv.at[0], twin)
    mine = pltpu.make_async_copy(own, shard(me), local_sem)
    mine.start()
    for d in range(1, pairs):
        slot = peer(pairs - d)
        remote(own, shard(slot), a_send.at[d - 1], a_recv.at[d - 1], slot).wait_recv()
        go(shard(slot), slot, t_send.at[d], t_recv.at[d], twin)
    for d in range(pairs):
        slot = lax.rem(pair + pairs - d, pairs) * 2 + 1 - core
        remote(own, shard(slot), t_send.at[d], t_recv.at[d], twin).wait_recv()
    mine.wait()
    return copies + lines + sent


def whole_kernel(
    lines, units, parts, capacity, rank_max,
    contrast, row_tile, row_block, row_rank, col_tile, col_block, col_rank,
    row_target, col_target, probes, level, label, weight, u_hbm, v_hbm,
    out,
    u_here, v_here, cells, own_cells, data,
    part, near_part, got_c, send_line, got_line, own,
    send_twin, got_twin, send_y, got_y, near, send_z, got_z,
    c_send, c_recv, l_send, l_recv, a_send, a_recv, t_send, t_recv, local_sem, u_sem, v_sem,
    x_send, x_recv, y_send, y_recv, z_send, z_recv, cells_sem, *gather
):
    me, core, side, step = place(lines)
    pairs = 2 * lines
    across = index_of(step, 1 - side, core)
    twin = index_of(step, side, 1 - core)
    barrier = pltpu.get_barrier_semaphore()
    for d in range(1, pairs):
        peer = lax.rem(me // 2 + d, pairs) * 2 + core
        pl.semaphore_signal(barrier, inc=1, device_id={"tile": peer}, device_id_type=MESH)
    pl.semaphore_signal(barrier, inc=1, device_id={"tile": twin}, device_id_type=MESH)
    u_copy = pltpu.make_async_copy(u_hbm, u_here, u_sem)
    v_copy = pltpu.make_async_copy(v_hbm, v_here, v_sem)
    u_copy.start()
    v_copy.start()
    cell_count = own_cells.shape[0]
    width = probes.shape[1] // cell_count
    size = cell_count // parts

    def fill(p):
        for b in range(p * size, (p + 1) * size):
            cut = pl.ds(b * width, width)
            scaling = cell_scaling(level[:, cut], label[:, cut], contrast, units)
            own_cells[b] = halves(probes[:, cut] * scaling).astype(BF16)

    pl.semaphore_wait(barrier, pairs)
    pending = gather_shards(
        lines, parts, fill, own_cells, cells, cells_sem, gather, step, side, core
    )
    u_copy.wait()
    v_copy.wait()

    def station_chunks(owners):
        tables = (row_tile, row_block, row_rank, row_target)
        return block_chunks(
            owners, tables, capacity, rank_max, part.shape[1], cells, v_here, u_here
        )

    pending += stations_phase(
        pairs, station_chunks, weight, data,
        part, near_part, got_c, send_line, got_line, own,
        c_send, c_recv, l_send, l_recv, a_send, a_recv, t_send, t_recv, local_sem,
    )
    chunk = near.shape[1]

    def chunks(owners):
        tables = (col_tile, col_block, col_rank, col_target)
        return block_chunks(owners, tables, capacity, rank_max, chunk, data, u_here, v_here)

    def target(k):
        return lax.rem(step + k + 1, lines)

    def twin_copy(far, k):
        return remote(
            send_twin.at[far, k], got_twin.at[far, k], x_send.at[far, k], x_recv.at[far, k], twin
        )

    def y_copy(k):
        return remote(send_y.at[k], got_y.at[k], y_send.at[k], y_recv.at[k], across)

    def z_copy(k):
        return remote(
            send_z.at[k], got_z.at[k], z_send.at[k], z_recv.at[k],
            index_of(target(k), side, core),
        )

    def one_target(k, _):
        there = target(k)
        first, second = chunks(
            [index_of(there, 1 - side, 1 - core), index_of(there, side, 1 - core)]
        )
        send_twin[0, k] = first.astype(BF16)
        twin_copy(0, k).start()
        send_twin[1, k] = second.astype(BF16)
        twin_copy(1, k).start()
        first, second = chunks([index_of(there, 1 - side, core), index_of(there, side, core)])
        twin_copy(0, k).wait_recv()
        send_y[k] = (first + got_twin[0, k].astype(F32)).astype(BF16)
        y_copy(k).start()
        twin_copy(1, k).wait_recv()
        near[k] = second + got_twin[1, k].astype(F32)

        @pl.when(k > 0)
        def _():
            y_copy(k - 1).wait_recv()
            send_z[k - 1] = (near[k - 1] + got_y[k - 1].astype(F32)).astype(BF16)
            z_copy(k - 1).start()

        return 0

    lax.fori_loop(0, lines, one_target, 0)
    y_copy(lines - 1).wait_recv()
    for k in range(lines - 1):
        z_copy(k).wait_recv()
    for b in range(chunk // 8):
        cut = pl.ds(b * width, width)
        band = slice(b * 8, (b + 1) * 8)
        piece = near[lines - 1, band] + got_y[lines - 1, band].astype(F32)
        for k in range(lines - 1):
            piece += got_z[k, band].astype(F32)
        out[:, cut] = piece * cell_scaling(level[:, cut], label[:, cut], contrast, units)
    for copy in pending:
        copy.wait_send()
    for k in range(lines):
        twin_copy(0, k).wait_send()
        twin_copy(1, k).wait_send()
        y_copy(k).wait_send()
        if k < lines - 1:
            z_copy(k).wait_send()


def params(number):
    return pltpu.CompilerParams(
        collective_id=number, has_side_effects=True, vmem_limit_bytes=VMEM_LIMIT
    )


VM = pl.BlockSpec(memory_space=pltpu.VMEM)
SM = pl.BlockSpec(memory_space=pltpu.SMEM)
ANY = pl.BlockSpec(memory_space=pl.ANY)


def shards(
    probes,
    level_set,
    unit_label,
    contrast,
    station_weight,
    u_factor,
    v_factor,
    col_owner,
    col_local,
    row_owner,
    row_local,
    tile_rank,
):
    peers = lax.axis_size("tile")
    lines = peers // 4
    own_index = lax.axis_index("tile")
    tiles, rank_max, width = u_factor.shape
    cell_total = probes.shape[1]
    cell_blocks = cell_total // width
    station_blocks = station_weight.shape[0] // (peers * width)
    units = contrast.shape[0]
    half = width // 2
    parts = 4 if cell_blocks % 4 == 0 else 1
    dma = pltpu.SemaphoreType.DMA

    capacity = max(2, 2 * tiles // peers)
    size = min(GROUP, capacity)

    def own_part(table):
        return lax.dynamic_slice_in_dim(table.reshape(-1), own_index * tiles, tiles)

    owner, local = own_part(col_owner), own_part(col_local)
    row_who, row_where = own_part(row_owner), own_part(row_local)
    ranks = own_part(tile_rank)
    col_take = owner * cell_blocks + local
    row_take = row_who * station_blocks + row_where

    number = jnp.arange(tiles, dtype=jnp.int32)
    rank_range = rank_max + 1

    def slots(owner, local, local_range, block, block_range):
        earlier = (owner[None, :] == owner[:, None]) & (number[None, :] < number[:, None])
        slot = owner * capacity + jnp.sum(earlier.astype(jnp.int32), axis=1)
        packed = ((number * block_range + block) * rank_range + ranks) * local_range + local
        held = jnp.arange(peers * capacity, dtype=jnp.int32)[:, None] == slot[None, :]
        packed = jnp.sum(jnp.where(held, packed[None, :], 0), axis=1)
        where = packed % local_range
        packed = packed // local_range
        rank = packed % rank_range
        packed = packed // rank_range
        target = where[:, None] * 8 + jnp.arange(8, dtype=jnp.int32)[None, :]
        target = target.reshape(peers * capacity // size, 1, size * 8)
        return packed // block_range, packed % block_range, rank, target

    row_tile, row_block, row_rank, row_target = slots(
        row_who, row_where, station_blocks, col_take, peers * cell_blocks
    )
    col_tile, col_block, col_rank, col_target = slots(
        owner, local, cell_blocks, row_take, peers * station_blocks
    )
    level = level_set.reshape(1, cell_total)
    label = unit_label.reshape(1, cell_total)
    weight = station_weight.reshape(1, -1)

    small = station_blocks * 8
    chunk = cell_blocks * 8
    pairs = peers // 2
    factors = pltpu.VMEM((tiles, rank_max, width), BF16)
    with jax.named_scope("hessian_kernel"):
        return pl.pallas_call(
            functools.partial(whole_kernel, lines, units, parts, capacity, rank_max),
            out_shape=jax.ShapeDtypeStruct(probes.shape, F32),
            in_specs=[SM] * 7 + [VM] * 6 + [ANY] * 2,
            out_specs=VM,
            scratch_shapes=[
                factors,
                factors,
                pltpu.VMEM((peers * cell_blocks, 16, half), BF16),
                pltpu.VMEM((cell_blocks, 16, half), BF16),
                pltpu.VMEM((peers * station_blocks, 16, half), BF16),
                pltpu.VMEM((pairs, small, width), F32),
                pltpu.VMEM((pairs, small, width), F32),
                pltpu.VMEM((pairs, small, width), F32),
                pltpu.VMEM((pairs - 1, small, width), BF16),
                pltpu.VMEM((pairs - 1, small, width), BF16),
                pltpu.VMEM((station_blocks, 16, half), BF16),
                pltpu.VMEM((2, lines, chunk, width), BF16),
                pltpu.VMEM((2, lines, chunk, width), BF16),
                pltpu.VMEM((lines, chunk, width), BF16),
                pltpu.VMEM((lines, chunk, width), BF16),
                pltpu.VMEM((lines, chunk, width), F32),
                pltpu.VMEM((lines - 1, chunk, width), BF16),
                pltpu.VMEM((lines - 1, chunk, width), BF16),
                dma((pairs,)),
                dma((pairs,)),
                dma((pairs - 1,)),
                dma((pairs - 1,)),
                dma((pairs - 1,)),
                dma((pairs - 1,)),
                dma((pairs,)),
                dma((pairs,)),
                dma,
                dma,
                dma,
                dma((2, lines)),
                dma((2, lines)),
                dma((lines,)),
                dma((lines,)),
                dma((lines - 1,)),
                dma((lines - 1,)),
                dma,
            ]
            + gather_sems(lines, parts),
            compiler_params=params(0),
        )(
            contrast, row_tile, row_block, row_rank, col_tile, col_block, col_rank,
            row_target, col_target, probes, level, label, weight, u_factor, v_factor,
        )


def solution(mesh):
    placed = (
        P(None, ("groups", "tile")),
        P(("groups", "tile")),
        P(("groups", "tile")),
        P("groups"),
        P("groups"),
        P(("groups", "tile"), None, None),
        P(("groups", "tile"), None, None),
        P("groups", None),
        P("groups"),
        P("groups", None),
        P("groups"),
        P("groups"),
    )
    return jax.shard_map(
        shards, mesh=mesh, in_specs=placed, out_specs=P(None, ("groups", "tile")), check_vma=False
    )
```

```python
import functools

import jax
import jax.numpy as jnp
from jax import lax
from jax.experimental import pallas as pl
from jax.experimental.pallas import tpu as pltpu
from jax.sharding import PartitionSpec as P

MESH = pl.DeviceIdType.MESH
VMEM_LIMIT = 56 * 1024 * 1024
GROUP = 8
F32 = jnp.float32
BF16 = jnp.bfloat16


def place(lines):
    me = lax.axis_index("tile")
    core = lax.rem(me, 2)
    side = lax.rem(me // 2, 2)
    step = me // 4
    return me, core, side, step


def index_of(step, side, core):
    return (step * 2 + side) * 2 + core


def remote(src, dst, send, recv, peer):
    return pltpu.make_async_remote_copy(
        src_ref=src,
        dst_ref=dst,
        send_sem=send,
        recv_sem=recv,
        device_id={"tile": peer},
        device_id_type=MESH,
    )


def gather_shards(lines, parts, fill, own, out, local_sem, sems, step, side, core):
    send_z, recv_z, send_y, recv_y, send_c, recv_c = sems
    me = index_of(step, side, core)
    across = index_of(step, 1 - side, core)
    twin = index_of(step, side, 1 - core)
    count = own.shape[0]
    size = count // parts
    started = []

    def at(slot, p):
        return out.at[pl.ds(slot * count + p * size, size)]

    def go(src, slot, p, send, recv, peer):
        copy = remote(src, at(slot, p), send, recv, peer)
        copy.start()
        started.append(copy)

    def arrived(slot, p, recv, peer):
        remote(at(slot, p), at(slot, p), recv, recv, peer).wait_recv()

    for p in range(parts):
        fill(p)
        piece = own.at[pl.ds(p * size, size)]
        go(piece, me, p, send_y.at[0, p], recv_y.at[0, p], across)
        for d in range(1, lines):
            peer = index_of(lax.rem(step + d, lines), side, core)
            go(piece, me, p, send_z.at[d - 1, p], recv_z.at[d - 1, p], peer)
    for p in range(parts):
        piece = own.at[pl.ds(p * size, size)]
        go(piece, me, p, send_c.at[0, p], recv_c.at[0, p], twin)
    mine = pltpu.make_async_copy(own, out.at[pl.ds(me * count, count)], local_sem)
    mine.start()

    for p in range(parts + 1):
        if p < parts:
            for k in range(1, lines):
                slot = index_of(lax.rem(step + lines - k, lines), side, core)
                arrived(slot, p, recv_z.at[k - 1, p], me)
                go(at(slot, p), slot, p, send_y.at[k, p], recv_y.at[k, p], across)
                go(at(slot, p), slot, p, send_c.at[k, p], recv_c.at[k, p], twin)
        if p >= 1:
            for k in range(lines):
                slot = index_of(lax.rem(step + lines - k, lines), 1 - side, core)
                arrived(slot, p - 1, recv_y.at[k, p - 1], across)
                far = lines + k
                go(
                    at(slot, p - 1), slot, p - 1,
                    send_c.at[far, p - 1], recv_c.at[far, p - 1], twin,
                )
    for p in range(parts):
        for k in range(lines):
            for far in range(2):
                where = 1 - side if far else side
                slot = index_of(lax.rem(step + lines - k, lines), where, 1 - core)
                arrived(slot, p, recv_c.at[far * lines + k, p], twin)
    mine.wait()
    return started


def gather_sems(lines, parts):
    dma = pltpu.SemaphoreType.DMA
    return [
        dma((lines - 1, parts)),
        dma((lines - 1, parts)),
        dma((lines, parts)),
        dma((lines, parts)),
        dma((2 * lines, parts)),
        dma((2 * lines, parts)),
    ]


def cell_scaling(level, label, contrast, units):
    picked = jnp.full(level.shape, contrast[0], F32)
    for unit in range(1, units):
        picked = jnp.where(label == unit, contrast[unit], picked)
    return picked / (1.0 + level * level)


def halves(block):
    half = block.shape[1] // 2
    return jnp.concatenate([block[:, :half], block[:, half:]], axis=0)


def bits_of(limit):
    return max(1, (limit - 1).bit_length())


def block_chunks(owners, tables, capacity, rank_max, chunk, source, inward, outward):
    codes, lane_block, shift, tile_shift = tables
    block_mask = (1 << (tile_shift - shift)) - 1
    size = min(GROUP, capacity)
    groups = capacity // size
    rows = size * rank_max
    lane = lax.broadcasted_iota(jnp.int32, (8, rows), 1)
    jobs = [(o, g) for o in owners for g in range(groups)]
    inners = []
    for o, g in jobs:
        pieces, factors = [], []
        for j in range(size):
            code = codes[o * capacity + g * size + j]
            block = source[(code >> shift) & block_mask].astype(F32)
            pieces.append(jnp.concatenate([block[:8], block[8:]], axis=1))
            factors.append(inward[code >> tile_shift])
        inners.append(
            lax.dot_general(
                jnp.concatenate(pieces, axis=0).astype(BF16),
                jnp.concatenate(factors, axis=0),
                (((1,), (1,)), ((), ())),
                preferred_element_type=F32,
            )
        )
    spread = []
    for (o, g), inner in zip(jobs, inners):
        compact = inner[:8]
        for j in range(1, size):
            compact = jnp.where(lane >= j * rank_max, inner[j * 8 : (j + 1) * 8], compact)
        where = jnp.broadcast_to(lane_block[o * groups + g], (8, rows))
        spread.append(
            jnp.concatenate(
                [jnp.where(where == b, compact, 0.0) for b in range(chunk // 8)], axis=0
            ).astype(BF16)
        )
    values = []
    for n in range(len(owners)):
        value = None
        for g in range(groups):
            s = owners[n] * capacity + g * size
            factors = jnp.concatenate(
                [outward[codes[s + j] >> tile_shift] for j in range(size)], axis=0
            )
            term = jnp.dot(spread[n * groups + g], factors, preferred_element_type=F32)
            value = term if value is None else value + term
        values.append(value)
    return values


def stations_phase(
    pairs, chunks, weight, out,
    part, near, got_c, send_line, got_line, own,
    c_send, c_recv, l_send, l_recv, a_send, a_recv, t_send, t_recv, local_sem
):
    me = lax.axis_index("tile")
    core = lax.rem(me, 2)
    pair = me // 2
    twin = pair * 2 + 1 - core
    count = own.shape[0]
    width = part.shape[2]

    def peer(d):
        return lax.rem(pair + d, pairs) * 2 + core

    def shard(slot):
        return out.at[pl.ds(slot * count, count)]

    def c_copy(i):
        return remote(part.at[i], got_c.at[i], c_send.at[i], c_recv.at[i], twin)

    def line(i):
        return remote(
            send_line.at[i], got_line.at[i], l_send.at[i], l_recv.at[i], peer(i + 1)
        )

    def one_pair(i, _):
        there = lax.rem(pair + i + 1, pairs) * 2
        first, second = chunks([there + 1 - core, there + core])
        part[i] = first
        c_copy(i).start()
        near[i] = second

        @pl.when(i > 0)
        def _():
            c_copy(i - 1).wait_recv()
            send_line[i - 1] = (near[i - 1] + got_c[i - 1]).astype(BF16)
            line(i - 1).start()

        return 0

    lax.fori_loop(0, pairs, one_pair, 0)
    c_copy(pairs - 1).wait_recv()
    total = near[pairs - 1] + got_c[pairs - 1]
    copies = [c_copy(i) for i in range(pairs)]
    lines = [line(i) for i in range(pairs - 1)]
    for i in range(pairs - 1):
        lines[i].wait_recv()
        total += got_line[i].astype(F32)
    for b in range(count):
        start = pl.multiple_of(me * (count * width) + b * width, width)
        factor = weight[:, pl.ds(start, width)]
        own[b] = halves(total[b * 8 : (b + 1) * 8] * factor).astype(BF16)
    sent = []

    def go(src, slot, send, recv, target):
        copy = remote(src, shard(slot), send, recv, target)
        copy.start()
        sent.append(copy)

    for d in range(1, pairs):
        go(own, me, a_send.at[d - 1], a_recv.at[d - 1], peer(d))
    go(own, me, t_send.at[0], t_recv.at[0], twin)
    mine = pltpu.make_async_copy(own, shard(me), local_sem)
    mine.start()
    for d in range(1, pairs):
        slot = peer(pairs - d)
        remote(own, shard(slot), a_send.at[d - 1], a_recv.at[d - 1], slot).wait_recv()
        go(shard(slot), slot, t_send.at[d], t_recv.at[d], twin)
    for d in range(pairs):
        slot = lax.rem(pair + pairs - d, pairs) * 2 + 1 - core
        remote(own, shard(slot), t_send.at[d], t_recv.at[d], twin).wait_recv()
    mine.wait()
    return copies + lines + sent


def whole_kernel(
    lines, units, parts, capacity, rank_max, row_shifts, col_shifts,
    contrast, row_codes, col_codes, row_lanes, col_lanes, probes, level, label, weight, u_hbm, v_hbm,
    out,
    u_here, v_here, cells, own_cells, data,
    part, near_part, got_c, send_line, got_line, own,
    send_twin, got_twin, send_y, got_y, near, send_z, got_z,
    c_send, c_recv, l_send, l_recv, a_send, a_recv, t_send, t_recv, local_sem, u_sem, v_sem,
    x_send, x_recv, y_send, y_recv, z_send, z_recv, cells_sem, *gather
):
    me, core, side, step = place(lines)
    pairs = 2 * lines
    across = index_of(step, 1 - side, core)
    twin = index_of(step, side, 1 - core)
    barrier = pltpu.get_barrier_semaphore()
    for d in range(1, pairs):
        peer = lax.rem(me // 2 + d, pairs) * 2 + core
        pl.semaphore_signal(barrier, inc=1, device_id={"tile": peer}, device_id_type=MESH)
    pl.semaphore_signal(barrier, inc=1, device_id={"tile": twin}, device_id_type=MESH)
    u_copy = pltpu.make_async_copy(u_hbm, u_here, u_sem)
    v_copy = pltpu.make_async_copy(v_hbm, v_here, v_sem)
    u_copy.start()
    v_copy.start()
    cell_count = own_cells.shape[0]
    width = probes.shape[1] // cell_count
    size = cell_count // parts

    def fill(p):
        for b in range(p * size, (p + 1) * size):
            cut = pl.ds(b * width, width)
            scaling = cell_scaling(level[:, cut], label[:, cut], contrast, units)
            own_cells[b] = halves(probes[:, cut] * scaling).astype(BF16)

    pl.semaphore_wait(barrier, pairs)
    pending = gather_shards(
        lines, parts, fill, own_cells, cells, cells_sem, gather, step, side, core
    )
    u_copy.wait()
    v_copy.wait()

    def station_chunks(owners):
        tables = (row_codes, row_lanes) + row_shifts
        return block_chunks(
            owners, tables, capacity, rank_max, part.shape[1], cells, v_here, u_here
        )

    pending += stations_phase(
        pairs, station_chunks, weight, data,
        part, near_part, got_c, send_line, got_line, own,
        c_send, c_recv, l_send, l_recv, a_send, a_recv, t_send, t_recv, local_sem,
    )
    chunk = near.shape[1]

    def chunks(owners):
        tables = (col_codes, col_lanes) + col_shifts
        return block_chunks(owners, tables, capacity, rank_max, chunk, data, u_here, v_here)

    def target(k):
        return lax.rem(step + k + 1, lines)

    def twin_copy(far, k):
        return remote(
            send_twin.at[far, k], got_twin.at[far, k], x_send.at[far, k], x_recv.at[far, k], twin
        )

    def y_copy(k):
        return remote(send_y.at[k], got_y.at[k], y_send.at[k], y_recv.at[k], across)

    def z_copy(k):
        return remote(
            send_z.at[k], got_z.at[k], z_send.at[k], z_recv.at[k],
            index_of(target(k), side, core),
        )

    def one_target(k, _):
        there = target(k)
        first, second = chunks(
            [index_of(there, 1 - side, 1 - core), index_of(there, side, 1 - core)]
        )
        send_twin[0, k] = first.astype(BF16)
        twin_copy(0, k).start()
        send_twin[1, k] = second.astype(BF16)
        twin_copy(1, k).start()
        first, second = chunks([index_of(there, 1 - side, core), index_of(there, side, core)])
        twin_copy(0, k).wait_recv()
        send_y[k] = (first + got_twin[0, k].astype(F32)).astype(BF16)
        y_copy(k).start()
        twin_copy(1, k).wait_recv()
        near[k] = second + got_twin[1, k].astype(F32)

        @pl.when(k > 0)
        def _():
            y_copy(k - 1).wait_recv()
            send_z[k - 1] = (near[k - 1] + got_y[k - 1].astype(F32)).astype(BF16)
            z_copy(k - 1).start()

        return 0

    lax.fori_loop(0, lines, one_target, 0)
    y_copy(lines - 1).wait_recv()
    for k in range(lines - 1):
        z_copy(k).wait_recv()
    for b in range(chunk // 8):
        cut = pl.ds(b * width, width)
        band = slice(b * 8, (b + 1) * 8)
        piece = near[lines - 1, band] + got_y[lines - 1, band].astype(F32)
        for k in range(lines - 1):
            piece += got_z[k, band].astype(F32)
        out[:, cut] = piece * cell_scaling(level[:, cut], label[:, cut], contrast, units)
    for copy in pending:
        copy.wait_send()
    for k in range(lines):
        twin_copy(0, k).wait_send()
        twin_copy(1, k).wait_send()
        y_copy(k).wait_send()
        if k < lines - 1:
            z_copy(k).wait_send()


def params(number):
    return pltpu.CompilerParams(
        collective_id=number, has_side_effects=True, vmem_limit_bytes=VMEM_LIMIT
    )


VM = pl.BlockSpec(memory_space=pltpu.VMEM)
SM = pl.BlockSpec(memory_space=pltpu.SMEM)
ANY = pl.BlockSpec(memory_space=pl.ANY)


def shards(
    probes,
    level_set,
    unit_label,
    contrast,
    station_weight,
    u_factor,
    v_factor,
    col_owner,
    col_local,
    row_owner,
    row_local,
    tile_rank,
):
    peers = lax.axis_size("tile")
    lines = peers // 4
    own_index = lax.axis_index("tile")
    tiles, rank_max, width = u_factor.shape
    cell_total = probes.shape[1]
    cell_blocks = cell_total // width
    station_blocks = station_weight.shape[0] // (peers * width)
    units = contrast.shape[0]
    half = width // 2
    parts = 4 if cell_blocks % 4 == 0 else 1
    dma = pltpu.SemaphoreType.DMA

    capacity = max(2, 2 * tiles // peers)
    size = min(GROUP, capacity)

    def own_part(table):
        return lax.dynamic_slice_in_dim(table.reshape(-1), own_index * tiles, tiles)

    owner, local = own_part(col_owner), own_part(col_local)
    row_who, row_where = own_part(row_owner), own_part(row_local)
    ranks = own_part(tile_rank)
    col_take = owner * cell_blocks + local
    row_take = row_who * station_blocks + row_where

    number = jnp.arange(tiles, dtype=jnp.int32)
    rank_bits = bits_of(rank_max + 1)

    def slots(owner, local, local_range, block, block_range):
        shift = rank_bits + bits_of(local_range)
        tile_shift = shift + bits_of(block_range)
        earlier = (owner[None, :] == owner[:, None]) & (number[None, :] < number[:, None])
        slot = owner * capacity + jnp.sum(earlier.astype(jnp.int32), axis=1)
        code = (number << tile_shift) | (block << shift) | (local << rank_bits) | ranks
        held = jnp.arange(peers * capacity, dtype=jnp.int32)[:, None] == slot[None, :]
        code = jnp.sum(jnp.where(held, code[None, :], 0), axis=1)
        rank = code & ((1 << rank_bits) - 1)
        where = (code >> rank_bits) & ((1 << (shift - rank_bits)) - 1)
        kept = jnp.arange(rank_max, dtype=jnp.int32)[None, :] < rank[:, None]
        lanes = jnp.where(kept, where[:, None], -1)
        lanes = lanes.reshape(peers * capacity // size, 1, size * rank_max)
        return code, lanes, (shift, tile_shift)

    row_codes, row_lanes, row_shifts = slots(
        row_who, row_where, station_blocks, col_take, peers * cell_blocks
    )
    col_codes, col_lanes, col_shifts = slots(
        owner, local, cell_blocks, row_take, peers * station_blocks
    )
    level = level_set.reshape(1, cell_total)
    label = unit_label.reshape(1, cell_total)
    weight = station_weight.reshape(1, -1)

    small = station_blocks * 8
    chunk = cell_blocks * 8
    pairs = peers // 2
    factors = pltpu.VMEM((tiles, rank_max, width), BF16)
    with jax.named_scope("hessian_kernel"):
        return pl.pallas_call(
            functools.partial(
                whole_kernel, lines, units, parts, capacity, rank_max, row_shifts, col_shifts
            ),
            out_shape=jax.ShapeDtypeStruct(probes.shape, F32),
            in_specs=[SM] * 3 + [VM] * 6 + [ANY] * 2,
            out_specs=VM,
            scratch_shapes=[
                factors,
                factors,
                pltpu.VMEM((peers * cell_blocks, 16, half), BF16),
                pltpu.VMEM((cell_blocks, 16, half), BF16),
                pltpu.VMEM((peers * station_blocks, 16, half), BF16),
                pltpu.VMEM((pairs, small, width), F32),
                pltpu.VMEM((pairs, small, width), F32),
                pltpu.VMEM((pairs, small, width), F32),
                pltpu.VMEM((pairs - 1, small, width), BF16),
                pltpu.VMEM((pairs - 1, small, width), BF16),
                pltpu.VMEM((station_blocks, 16, half), BF16),
                pltpu.VMEM((2, lines, chunk, width), BF16),
                pltpu.VMEM((2, lines, chunk, width), BF16),
                pltpu.VMEM((lines, chunk, width), BF16),
                pltpu.VMEM((lines, chunk, width), BF16),
                pltpu.VMEM((lines, chunk, width), F32),
                pltpu.VMEM((lines - 1, chunk, width), BF16),
                pltpu.VMEM((lines - 1, chunk, width), BF16),
                dma((pairs,)),
                dma((pairs,)),
                dma((pairs - 1,)),
                dma((pairs - 1,)),
                dma((pairs - 1,)),
                dma((pairs - 1,)),
                dma((pairs,)),
                dma((pairs,)),
                dma,
                dma,
                dma,
                dma((2, lines)),
                dma((2, lines)),
                dma((lines,)),
                dma((lines,)),
                dma((lines - 1,)),
                dma((lines - 1,)),
                dma,
            ]
            + gather_sems(lines, parts),
            compiler_params=params(0),
        )(
            contrast, row_codes, col_codes, row_lanes, col_lanes, probes, level, label, weight, u_factor, v_factor,
        )


def solution(mesh):
    placed = (
        P(None, ("groups", "tile")),
        P(("groups", "tile")),
        P(("groups", "tile")),
        P("groups"),
        P("groups"),
        P(("groups", "tile"), None, None),
        P(("groups", "tile"), None, None),
        P("groups", None),
        P("groups"),
        P("groups", None),
        P("groups"),
        P("groups"),
    )
    return jax.shard_map(
        shards, mesh=mesh, in_specs=placed, out_specs=P(None, ("groups", "tile")), check_vma=False
    )
```

```python
import functools

import jax
import jax.numpy as jnp
from jax import lax
from jax.experimental import pallas as pl
from jax.experimental.pallas import tpu as pltpu
from jax.sharding import PartitionSpec as P

MESH = pl.DeviceIdType.MESH
VMEM_LIMIT = 56 * 1024 * 1024
GROUP = 8
F32 = jnp.float32
BF16 = jnp.bfloat16


def place(lines):
    me = lax.axis_index("tile")
    core = lax.rem(me, 2)
    side = lax.rem(me // 2, 2)
    step = me // 4
    return me, core, side, step


def crossed(step, turn, lines):
    result, weight = 0, 1
    while weight < lines:
        one, two = lax.rem(step // weight, 2), (turn // weight) % 2
        result += (one + two - 2 * one * two) * weight
        weight *= 2
    return result


def index_of(step, side, core):
    return (step * 2 + side) * 2 + core


def remote(src, dst, send, recv, peer):
    return pltpu.make_async_remote_copy(
        src_ref=src,
        dst_ref=dst,
        send_sem=send,
        recv_sem=recv,
        device_id={"tile": peer},
        device_id_type=MESH,
    )


def gather_shards(lines, parts, fill, own, out, local_sem, sems, step, side, core):
    send_z, recv_z, send_y, recv_y, send_c, recv_c = sems
    me = index_of(step, side, core)
    across = index_of(step, 1 - side, core)
    twin = index_of(step, side, 1 - core)
    count = own.shape[0]
    size = count // parts
    started = []

    def at(slot, p):
        return out.at[pl.ds(slot * count + p * size, size)]

    def go(src, slot, p, send, recv, peer):
        copy = remote(src, at(slot, p), send, recv, peer)
        copy.start()
        started.append(copy)

    def arrived(slot, p, recv, peer):
        remote(at(slot, p), at(slot, p), recv, recv, peer).wait_recv()

    for p in range(parts):
        fill(p)
        piece = own.at[pl.ds(p * size, size)]
        go(piece, me, p, send_y.at[0, p], recv_y.at[0, p], across)
        for d in reversed(range(1, lines)):
            peer = index_of(crossed(step, d, lines), side, core)
            go(piece, me, p, send_z.at[d - 1, p], recv_z.at[d - 1, p], peer)
    for p in range(parts):
        piece = own.at[pl.ds(p * size, size)]
        go(piece, me, p, send_c.at[0, p], recv_c.at[0, p], twin)
    mine = pltpu.make_async_copy(own, out.at[pl.ds(me * count, count)], local_sem)
    mine.start()

    for p in range(parts + 1):
        if p < parts:
            for k in range(1, lines):
                slot = index_of(crossed(step, k, lines), side, core)
                arrived(slot, p, recv_z.at[k - 1, p], me)
                go(at(slot, p), slot, p, send_y.at[k, p], recv_y.at[k, p], across)
                go(at(slot, p), slot, p, send_c.at[k, p], recv_c.at[k, p], twin)
        if p >= 1:
            for k in range(lines):
                slot = index_of(crossed(step, k, lines), 1 - side, core)
                arrived(slot, p - 1, recv_y.at[k, p - 1], across)
                far = lines + k
                go(
                    at(slot, p - 1), slot, p - 1,
                    send_c.at[far, p - 1], recv_c.at[far, p - 1], twin,
                )
    for p in range(parts):
        for k in range(lines):
            for far in range(2):
                where = 1 - side if far else side
                slot = index_of(crossed(step, k, lines), where, 1 - core)
                arrived(slot, p, recv_c.at[far * lines + k, p], twin)
    mine.wait()
    return started


def gather_sems(lines, parts):
    dma = pltpu.SemaphoreType.DMA
    return [
        dma((lines - 1, parts)),
        dma((lines - 1, parts)),
        dma((lines, parts)),
        dma((lines, parts)),
        dma((2 * lines, parts)),
        dma((2 * lines, parts)),
    ]


def cell_scaling(level, label, contrast, units):
    picked = jnp.full(level.shape, contrast[0], F32)
    for unit in range(1, units):
        picked = jnp.where(label == unit, contrast[unit], picked)
    return picked / (1.0 + level * level)


def halves(block):
    half = block.shape[1] // 2
    return jnp.concatenate([block[:, :half], block[:, half:]], axis=0)


def bits_of(limit):
    return max(1, (limit - 1).bit_length())


def block_chunks(owners, tables, capacity, rank_max, chunk, source, inward, outward):
    codes, lane_block, shift, tile_shift = tables
    block_mask = (1 << (tile_shift - shift)) - 1
    size = min(GROUP, capacity)
    groups = capacity // size
    rows = size * rank_max
    lane = lax.broadcasted_iota(jnp.int32, (8, rows), 1)
    jobs = [(o, g) for o in owners for g in range(groups)]
    inners = []
    for o, g in jobs:
        pieces, factors = [], []
        for j in range(size):
            code = codes[o * capacity + g * size + j]
            block = source[(code >> shift) & block_mask].astype(F32)
            pieces.append(jnp.concatenate([block[:8], block[8:]], axis=1))
            factors.append(inward[code >> tile_shift])
        inners.append(
            lax.dot_general(
                jnp.concatenate(pieces, axis=0).astype(BF16),
                jnp.concatenate(factors, axis=0),
                (((1,), (1,)), ((), ())),
                preferred_element_type=F32,
            )
        )
    spread = []
    for (o, g), inner in zip(jobs, inners):
        compact = inner[:8]
        for j in range(1, size):
            compact = jnp.where(lane >= j * rank_max, inner[j * 8 : (j + 1) * 8], compact)
        where = jnp.broadcast_to(lane_block[o * groups + g], (8, rows))
        spread.append(
            jnp.concatenate(
                [jnp.where(where == b, compact, 0.0) for b in range(chunk // 8)], axis=0
            ).astype(BF16)
        )
    values = []
    for n in range(len(owners)):
        value = None
        for g in range(groups):
            s = owners[n] * capacity + g * size
            factors = jnp.concatenate(
                [outward[codes[s + j] >> tile_shift] for j in range(size)], axis=0
            )
            term = jnp.dot(spread[n * groups + g], factors, preferred_element_type=F32)
            value = term if value is None else value + term
        values.append(value)
    return values


def stations_phase(
    pairs, chunks, weight, out,
    part, near, got_c, send_line, got_line, own,
    c_send, c_recv, l_send, l_recv, a_send, a_recv, t_send, t_recv, local_sem
):
    me = lax.axis_index("tile")
    core = lax.rem(me, 2)
    pair = me // 2
    twin = pair * 2 + 1 - core
    count = own.shape[0]
    width = part.shape[2]

    def peer(d):
        return lax.rem(pair + d, pairs) * 2 + core

    def shard(slot):
        return out.at[pl.ds(slot * count, count)]

    def c_copy(i):
        return remote(part.at[i], got_c.at[i], c_send.at[i], c_recv.at[i], twin)

    def line(i):
        return remote(
            send_line.at[i], got_line.at[i], l_send.at[i], l_recv.at[i], peer(i + 1)
        )

    def one_pair(i, _):
        there = lax.rem(pair + i + 1, pairs) * 2
        first, second = chunks([there + 1 - core, there + core])
        part[i] = first
        c_copy(i).start()
        near[i] = second

        @pl.when(i > 0)
        def _():
            c_copy(i - 1).wait_recv()
            send_line[i - 1] = (near[i - 1] + got_c[i - 1]).astype(BF16)
            line(i - 1).start()

        return 0

    lax.fori_loop(0, pairs, one_pair, 0)
    c_copy(pairs - 1).wait_recv()
    total = near[pairs - 1] + got_c[pairs - 1]
    copies = [c_copy(i) for i in range(pairs)]
    lines = [line(i) for i in range(pairs - 1)]
    for i in range(pairs - 1):
        lines[i].wait_recv()
        total += got_line[i].astype(F32)
    for b in range(count):
        start = pl.multiple_of(me * (count * width) + b * width, width)
        factor = weight[:, pl.ds(start, width)]
        own[b] = halves(total[b * 8 : (b + 1) * 8] * factor).astype(BF16)
    sent = []

    def go(src, slot, send, recv, target):
        copy = remote(src, shard(slot), send, recv, target)
        copy.start()
        sent.append(copy)

    for d in range(1, pairs):
        go(own, me, a_send.at[d - 1], a_recv.at[d - 1], peer(d))
    go(own, me, t_send.at[0], t_recv.at[0], twin)
    mine = pltpu.make_async_copy(own, shard(me), local_sem)
    mine.start()
    for d in range(1, pairs):
        slot = peer(pairs - d)
        remote(own, shard(slot), a_send.at[d - 1], a_recv.at[d - 1], slot).wait_recv()
        go(shard(slot), slot, t_send.at[d], t_recv.at[d], twin)
    for d in range(pairs):
        slot = lax.rem(pair + pairs - d, pairs) * 2 + 1 - core
        remote(own, shard(slot), t_send.at[d], t_recv.at[d], twin).wait_recv()
    mine.wait()
    return copies + lines + sent


def whole_kernel(
    lines, units, parts, capacity, rank_max, row_shifts, col_shifts,
    contrast, row_codes, col_codes, row_lanes, col_lanes, probes, level, label, weight, u_hbm, v_hbm,
    out,
    u_here, v_here, cells, own_cells, data,
    part, near_part, got_c, send_line, got_line, own,
    send_twin, got_twin, send_y, got_y, near, send_z, got_z,
    c_send, c_recv, l_send, l_recv, a_send, a_recv, t_send, t_recv, local_sem, u_sem, v_sem,
    x_send, x_recv, y_send, y_recv, z_send, z_recv, cells_sem, *gather
):
    me, core, side, step = place(lines)
    pairs = 2 * lines
    across = index_of(step, 1 - side, core)
    twin = index_of(step, side, 1 - core)
    barrier = pltpu.get_barrier_semaphore()
    for d in range(1, pairs):
        peer = lax.rem(me // 2 + d, pairs) * 2 + core
        pl.semaphore_signal(barrier, inc=1, device_id={"tile": peer}, device_id_type=MESH)
    pl.semaphore_signal(barrier, inc=1, device_id={"tile": twin}, device_id_type=MESH)
    u_copy = pltpu.make_async_copy(u_hbm, u_here, u_sem)
    v_copy = pltpu.make_async_copy(v_hbm, v_here, v_sem)
    u_copy.start()
    v_copy.start()
    cell_count = own_cells.shape[0]
    width = probes.shape[1] // cell_count
    size = cell_count // parts

    def fill(p):
        for b in range(p * size, (p + 1) * size):
            cut = pl.ds(b * width, width)
            scaling = cell_scaling(level[:, cut], label[:, cut], contrast, units)
            own_cells[b] = halves(probes[:, cut] * scaling).astype(BF16)

    pl.semaphore_wait(barrier, pairs)
    pending = gather_shards(
        lines, parts, fill, own_cells, cells, cells_sem, gather, step, side, core
    )
    u_copy.wait()
    v_copy.wait()

    def station_chunks(owners):
        tables = (row_codes, row_lanes) + row_shifts
        return block_chunks(
            owners, tables, capacity, rank_max, part.shape[1], cells, v_here, u_here
        )

    pending += stations_phase(
        pairs, station_chunks, weight, data,
        part, near_part, got_c, send_line, got_line, own,
        c_send, c_recv, l_send, l_recv, a_send, a_recv, t_send, t_recv, local_sem,
    )
    chunk = near.shape[1]

    def chunks(owners):
        tables = (col_codes, col_lanes) + col_shifts
        return block_chunks(owners, tables, capacity, rank_max, chunk, data, u_here, v_here)

    def target(k):
        return crossed(step, lines - 1 - k, lines)

    def twin_copy(far, k):
        return remote(
            send_twin.at[far, k], got_twin.at[far, k], x_send.at[far, k], x_recv.at[far, k], twin
        )

    def y_copy(k):
        return remote(send_y.at[k], got_y.at[k], y_send.at[k], y_recv.at[k], across)

    def z_copy(k):
        return remote(
            send_z.at[k], got_z.at[k], z_send.at[k], z_recv.at[k],
            index_of(target(k), side, core),
        )

    def one_target(k, _):
        there = target(k)
        first, second = chunks(
            [index_of(there, 1 - side, 1 - core), index_of(there, side, 1 - core)]
        )
        send_twin[0, k] = first.astype(BF16)
        twin_copy(0, k).start()
        send_twin[1, k] = second.astype(BF16)
        twin_copy(1, k).start()
        first, second = chunks([index_of(there, 1 - side, core), index_of(there, side, core)])
        twin_copy(0, k).wait_recv()
        send_y[k] = (first + got_twin[0, k].astype(F32)).astype(BF16)
        y_copy(k).start()
        twin_copy(1, k).wait_recv()
        near[k] = second + got_twin[1, k].astype(F32)

        @pl.when(k > 0)
        def _():
            y_copy(k - 1).wait_recv()
            send_z[k - 1] = (near[k - 1] + got_y[k - 1].astype(F32)).astype(BF16)
            z_copy(k - 1).start()

        return 0

    lax.fori_loop(0, lines, one_target, 0)
    y_copy(lines - 1).wait_recv()
    for k in range(lines - 1):
        z_copy(k).wait_recv()
    for b in range(chunk // 8):
        cut = pl.ds(b * width, width)
        band = slice(b * 8, (b + 1) * 8)
        piece = near[lines - 1, band] + got_y[lines - 1, band].astype(F32)
        for k in range(lines - 1):
            piece += got_z[k, band].astype(F32)
        out[:, cut] = piece * cell_scaling(level[:, cut], label[:, cut], contrast, units)
    for copy in pending:
        copy.wait_send()
    for k in range(lines):
        twin_copy(0, k).wait_send()
        twin_copy(1, k).wait_send()
        y_copy(k).wait_send()
        if k < lines - 1:
            z_copy(k).wait_send()


def params(number):
    return pltpu.CompilerParams(
        collective_id=number, has_side_effects=True, vmem_limit_bytes=VMEM_LIMIT
    )


VM = pl.BlockSpec(memory_space=pltpu.VMEM)
SM = pl.BlockSpec(memory_space=pltpu.SMEM)
ANY = pl.BlockSpec(memory_space=pl.ANY)


def shards(
    probes,
    level_set,
    unit_label,
    contrast,
    station_weight,
    u_factor,
    v_factor,
    col_owner,
    col_local,
    row_owner,
    row_local,
    tile_rank,
):
    peers = lax.axis_size("tile")
    lines = peers // 4
    own_index = lax.axis_index("tile")
    tiles, rank_max, width = u_factor.shape
    cell_total = probes.shape[1]
    cell_blocks = cell_total // width
    station_blocks = station_weight.shape[0] // (peers * width)
    units = contrast.shape[0]
    half = width // 2
    parts = 4 if cell_blocks % 4 == 0 else 1
    dma = pltpu.SemaphoreType.DMA

    capacity = max(2, 2 * tiles // peers)
    size = min(GROUP, capacity)

    def own_part(table):
        return lax.dynamic_slice_in_dim(table.reshape(-1), own_index * tiles, tiles)

    owner, local = own_part(col_owner), own_part(col_local)
    row_who, row_where = own_part(row_owner), own_part(row_local)
    ranks = own_part(tile_rank)
    col_take = owner * cell_blocks + local
    row_take = row_who * station_blocks + row_where

    number = jnp.arange(tiles, dtype=jnp.int32)
    rank_bits = bits_of(rank_max + 1)

    def slots(owner, local, local_range, block, block_range):
        shift = rank_bits + bits_of(local_range)
        tile_shift = shift + bits_of(block_range)
        earlier = (owner[None, :] == owner[:, None]) & (number[None, :] < number[:, None])
        slot = owner * capacity + jnp.sum(earlier.astype(jnp.int32), axis=1)
        code = (number << tile_shift) | (block << shift) | (local << rank_bits) | ranks
        held = jnp.arange(peers * capacity, dtype=jnp.int32)[:, None] == slot[None, :]
        code = jnp.sum(jnp.where(held, code[None, :], 0), axis=1)
        rank = code & ((1 << rank_bits) - 1)
        where = (code >> rank_bits) & ((1 << (shift - rank_bits)) - 1)
        kept = jnp.arange(rank_max, dtype=jnp.int32)[None, :] < rank[:, None]
        lanes = jnp.where(kept, where[:, None], -1)
        lanes = lanes.reshape(peers * capacity // size, 1, size * rank_max)
        return code, lanes, (shift, tile_shift)

    row_codes, row_lanes, row_shifts = slots(
        row_who, row_where, station_blocks, col_take, peers * cell_blocks
    )
    col_codes, col_lanes, col_shifts = slots(
        owner, local, cell_blocks, row_take, peers * station_blocks
    )
    level = level_set.reshape(1, cell_total)
    label = unit_label.reshape(1, cell_total)
    weight = station_weight.reshape(1, -1)

    small = station_blocks * 8
    chunk = cell_blocks * 8
    pairs = peers // 2
    factors = pltpu.VMEM((tiles, rank_max, width), BF16)
    with jax.named_scope("hessian_kernel"):
        return pl.pallas_call(
            functools.partial(
                whole_kernel, lines, units, parts, capacity, rank_max, row_shifts, col_shifts
            ),
            out_shape=jax.ShapeDtypeStruct(probes.shape, F32),
            in_specs=[SM] * 3 + [VM] * 6 + [ANY] * 2,
            out_specs=VM,
            scratch_shapes=[
                factors,
                factors,
                pltpu.VMEM((peers * cell_blocks, 16, half), BF16),
                pltpu.VMEM((cell_blocks, 16, half), BF16),
                pltpu.VMEM((peers * station_blocks, 16, half), BF16),
                pltpu.VMEM((pairs, small, width), F32),
                pltpu.VMEM((pairs, small, width), F32),
                pltpu.VMEM((pairs, small, width), F32),
                pltpu.VMEM((pairs - 1, small, width), BF16),
                pltpu.VMEM((pairs - 1, small, width), BF16),
                pltpu.VMEM((station_blocks, 16, half), BF16),
                pltpu.VMEM((2, lines, chunk, width), BF16),
                pltpu.VMEM((2, lines, chunk, width), BF16),
                pltpu.VMEM((lines, chunk, width), BF16),
                pltpu.VMEM((lines, chunk, width), BF16),
                pltpu.VMEM((lines, chunk, width), F32),
                pltpu.VMEM((lines - 1, chunk, width), BF16),
                pltpu.VMEM((lines - 1, chunk, width), BF16),
                dma((pairs,)),
                dma((pairs,)),
                dma((pairs - 1,)),
                dma((pairs - 1,)),
                dma((pairs - 1,)),
                dma((pairs - 1,)),
                dma((pairs,)),
                dma((pairs,)),
                dma,
                dma,
                dma,
                dma((2, lines)),
                dma((2, lines)),
                dma((lines,)),
                dma((lines,)),
                dma((lines - 1,)),
                dma((lines - 1,)),
                dma,
            ]
            + gather_sems(lines, parts),
            compiler_params=params(0),
        )(
            contrast, row_codes, col_codes, row_lanes, col_lanes, probes, level, label, weight, u_factor, v_factor,
        )


def solution(mesh):
    placed = (
        P(None, ("groups", "tile")),
        P(("groups", "tile")),
        P(("groups", "tile")),
        P("groups"),
        P("groups"),
        P(("groups", "tile"), None, None),
        P(("groups", "tile"), None, None),
        P("groups", None),
        P("groups"),
        P("groups", None),
        P("groups"),
        P("groups"),
    )
    return jax.shard_map(
        shards, mesh=mesh, in_specs=placed, out_specs=P(None, ("groups", "tile")), check_vma=False
    )
```

```python
import functools

import jax
import jax.numpy as jnp
from jax import lax
from jax.experimental import pallas as pl
from jax.experimental.pallas import tpu as pltpu
from jax.sharding import PartitionSpec as P

MESH = pl.DeviceIdType.MESH
VMEM_LIMIT = 56 * 1024 * 1024
GROUP = 8
F32 = jnp.float32
BF16 = jnp.bfloat16


def place(lines):
    me = lax.axis_index("tile")
    core = lax.rem(me, 2)
    side = lax.rem(me // 2, 2)
    step = me // 4
    return me, core, side, step


def index_of(step, side, core):
    return (step * 2 + side) * 2 + core


def remote(src, dst, send, recv, peer):
    return pltpu.make_async_remote_copy(
        src_ref=src,
        dst_ref=dst,
        send_sem=send,
        recv_sem=recv,
        device_id={"tile": peer},
        device_id_type=MESH,
    )


def gather_shards(lines, parts, own, out, local_sem, sems, step, side, core):
    send_z, recv_z, send_y, recv_y, send_c, recv_c = sems
    me = index_of(step, side, core)
    across = index_of(step, 1 - side, core)
    twin = index_of(step, side, 1 - core)
    count = own.shape[0]
    size = count // parts
    started = []

    def at(slot, p):
        return out.at[pl.ds(slot * count + p * size, size)]

    def go(src, slot, p, send, recv, peer):
        copy = remote(src, at(slot, p), send, recv, peer)
        copy.start()
        started.append(copy)

    def arrived(slot, p, recv, peer):
        remote(at(slot, p), at(slot, p), recv, recv, peer).wait_recv()

    for p in range(parts):
        piece = own.at[pl.ds(p * size, size)]
        go(piece, me, p, send_y.at[0, p], recv_y.at[0, p], across)
        for d in range(1, lines):
            peer = index_of(lax.rem(step + d, lines), side, core)
            go(piece, me, p, send_z.at[d - 1, p], recv_z.at[d - 1, p], peer)
    for p in range(parts):
        piece = own.at[pl.ds(p * size, size)]
        go(piece, me, p, send_c.at[0, p], recv_c.at[0, p], twin)
    mine = pltpu.make_async_copy(own, out.at[pl.ds(me * count, count)], local_sem)
    mine.start()

    for p in range(parts + 1):
        if p < parts:
            for k in range(1, lines):
                slot = index_of(lax.rem(step + lines - k, lines), side, core)
                arrived(slot, p, recv_z.at[k - 1, p], me)
                go(at(slot, p), slot, p, send_y.at[k, p], recv_y.at[k, p], across)
                go(at(slot, p), slot, p, send_c.at[k, p], recv_c.at[k, p], twin)
        if p >= 1:
            for k in range(lines):
                slot = index_of(lax.rem(step + lines - k, lines), 1 - side, core)
                arrived(slot, p - 1, recv_y.at[k, p - 1], across)
                far = lines + k
                go(
                    at(slot, p - 1), slot, p - 1,
                    send_c.at[far, p - 1], recv_c.at[far, p - 1], twin,
                )
    for p in range(parts):
        for k in range(lines):
            for far in range(2):
                where = 1 - side if far else side
                slot = index_of(lax.rem(step + lines - k, lines), where, 1 - core)
                arrived(slot, p, recv_c.at[far * lines + k, p], twin)
    mine.wait()
    return started


def gather_sems(lines, parts):
    dma = pltpu.SemaphoreType.DMA
    return [
        dma((lines - 1, parts)),
        dma((lines - 1, parts)),
        dma((lines, parts)),
        dma((lines, parts)),
        dma((2 * lines, parts)),
        dma((2 * lines, parts)),
    ]


def cell_scaling(level, label, contrast, units):
    picked = jnp.full(level.shape, contrast[0], F32)
    for unit in range(1, units):
        picked = jnp.where(label == unit, contrast[unit], picked)
    return picked / (1.0 + level * level)


def halves(block):
    half = block.shape[1] // 2
    return jnp.concatenate([block[:, :half], block[:, half:]], axis=0)


def bits_of(limit):
    return max(1, (limit - 1).bit_length())


def block_chunks(owners, tables, capacity, rank_max, chunk, source, inward, outward):
    codes, lane_block, shift, tile_shift = tables
    block_mask = (1 << (tile_shift - shift)) - 1
    size = min(GROUP, capacity)
    groups = capacity // size
    rows = size * rank_max
    lane = lax.broadcasted_iota(jnp.int32, (8, rows), 1)
    jobs = [(o, g) for o in owners for g in range(groups)]
    inners = []
    for o, g in jobs:
        pieces, factors = [], []
        for j in range(size):
            code = codes[o * capacity + g * size + j]
            block = source[(code >> shift) & block_mask].astype(F32)
            pieces.append(jnp.concatenate([block[:8], block[8:]], axis=1))
            factors.append(inward[code >> tile_shift])
        inners.append(
            lax.dot_general(
                jnp.concatenate(pieces, axis=0).astype(BF16),
                jnp.concatenate(factors, axis=0),
                (((1,), (1,)), ((), ())),
                preferred_element_type=F32,
            )
        )
    spread = []
    for (o, g), inner in zip(jobs, inners):
        compact = inner[:8]
        for j in range(1, size):
            compact = jnp.where(lane >= j * rank_max, inner[j * 8 : (j + 1) * 8], compact)
        where = jnp.broadcast_to(lane_block[o * groups + g], (8, rows))
        spread.append(
            jnp.concatenate(
                [jnp.where(where == b, compact, 0.0) for b in range(chunk // 8)], axis=0
            ).astype(BF16)
        )
    values = []
    for n in range(len(owners)):
        value = None
        for g in range(groups):
            s = owners[n] * capacity + g * size
            factors = jnp.concatenate(
                [outward[codes[s + j] >> tile_shift] for j in range(size)], axis=0
            )
            term = jnp.dot(spread[n * groups + g], factors, preferred_element_type=F32)
            value = term if value is None else value + term
        values.append(value)
    return values


def stations_phase(
    pairs, chunks, weight, out,
    part, near, got_c, send_line, got_line, own,
    c_send, c_recv, l_send, l_recv, a_send, a_recv, t_send, t_recv, local_sem
):
    me = lax.axis_index("tile")
    core = lax.rem(me, 2)
    pair = me // 2
    twin = pair * 2 + 1 - core
    count = own.shape[0]
    width = part.shape[2]

    def peer(d):
        return lax.rem(pair + d, pairs) * 2 + core

    def shard(slot):
        return out.at[pl.ds(slot * count, count)]

    def c_copy(i):
        return remote(part.at[i], got_c.at[i], c_send.at[i], c_recv.at[i], twin)

    def line(i):
        return remote(
            send_line.at[i], got_line.at[i], l_send.at[i], l_recv.at[i], peer(i + 1)
        )

    def one_pair(i, _):
        there = lax.rem(pair + i + 1, pairs) * 2
        first, second = chunks([there + 1 - core, there + core])
        part[i] = first
        c_copy(i).start()
        near[i] = second

        @pl.when(i > 0)
        def _():
            c_copy(i - 1).wait_recv()
            send_line[i - 1] = (near[i - 1] + got_c[i - 1]).astype(BF16)
            line(i - 1).start()

        return 0

    lax.fori_loop(0, pairs, one_pair, 0)
    c_copy(pairs - 1).wait_recv()
    total = near[pairs - 1] + got_c[pairs - 1]
    copies = [c_copy(i) for i in range(pairs)]
    lines = [line(i) for i in range(pairs - 1)]
    for i in range(pairs - 1):
        lines[i].wait_recv()
        total += got_line[i].astype(F32)
    for b in range(count):
        start = pl.multiple_of(me * (count * width) + b * width, width)
        factor = weight[:, pl.ds(start, width)]
        own[b] = halves(total[b * 8 : (b + 1) * 8] * factor).astype(BF16)
    sent = []

    def go(src, slot, send, recv, target):
        copy = remote(src, shard(slot), send, recv, target)
        copy.start()
        sent.append(copy)

    for d in range(1, pairs):
        go(own, me, a_send.at[d - 1], a_recv.at[d - 1], peer(d))
    go(own, me, t_send.at[0], t_recv.at[0], twin)
    mine = pltpu.make_async_copy(own, shard(me), local_sem)
    mine.start()
    for d in range(1, pairs):
        slot = peer(pairs - d)
        remote(own, shard(slot), a_send.at[d - 1], a_recv.at[d - 1], slot).wait_recv()
        go(shard(slot), slot, t_send.at[d], t_recv.at[d], twin)
    for d in range(pairs):
        slot = lax.rem(pair + pairs - d, pairs) * 2 + 1 - core
        remote(own, shard(slot), t_send.at[d], t_recv.at[d], twin).wait_recv()
    mine.wait()
    return copies + lines + sent


def whole_kernel(
    lines, units, parts, capacity, rank_max, row_shifts, col_shifts,
    contrast, row_codes, col_codes, row_lanes, col_lanes, probes, level, label, weight, u_hbm, v_hbm,
    out,
    u_here, v_here, cells, own_cells, data,
    part, near_part, got_c, send_line, got_line, own,
    send_twin, got_twin, send_y, got_y, near, send_z, got_z,
    c_send, c_recv, l_send, l_recv, a_send, a_recv, t_send, t_recv, local_sem, u_sem, v_sem,
    x_send, x_recv, y_send, y_recv, z_send, z_recv, cells_sem, *gather
):
    me, core, side, step = place(lines)
    pairs = 2 * lines
    across = index_of(step, 1 - side, core)
    twin = index_of(step, side, 1 - core)
    barrier = pltpu.get_barrier_semaphore()
    for d in range(1, pairs):
        peer = lax.rem(me // 2 + d, pairs) * 2 + core
        pl.semaphore_signal(barrier, inc=1, device_id={"tile": peer}, device_id_type=MESH)
    pl.semaphore_signal(barrier, inc=1, device_id={"tile": twin}, device_id_type=MESH)
    u_copy = pltpu.make_async_copy(u_hbm, u_here, u_sem)
    v_copy = pltpu.make_async_copy(v_hbm, v_here, v_sem)
    u_copy.start()
    v_copy.start()
    cell_count = own_cells.shape[0]
    width = probes.shape[1] // cell_count
    size = cell_count // parts

    def fill(p):
        for b in range(p * size, (p + 1) * size):
            cut = pl.ds(b * width, width)
            scaling = cell_scaling(level[:, cut], label[:, cut], contrast, units)
            own_cells[b] = halves(probes[:, cut] * scaling).astype(BF16)

    for p in range(parts):
        fill(p)
    pl.semaphore_wait(barrier, pairs)
    pending = gather_shards(
        lines, parts, own_cells, cells, cells_sem, gather, step, side, core
    )
    u_copy.wait()
    v_copy.wait()

    def station_chunks(owners):
        tables = (row_codes, row_lanes) + row_shifts
        return block_chunks(
            owners, tables, capacity, rank_max, part.shape[1], cells, v_here, u_here
        )

    pending += stations_phase(
        pairs, station_chunks, weight, data,
        part, near_part, got_c, send_line, got_line, own,
        c_send, c_recv, l_send, l_recv, a_send, a_recv, t_send, t_recv, local_sem,
    )
    chunk = near.shape[1]

    def chunks(owners):
        tables = (col_codes, col_lanes) + col_shifts
        return block_chunks(owners, tables, capacity, rank_max, chunk, data, u_here, v_here)

    def target(k):
        return lax.rem(step + k + 1, lines)

    def twin_copy(far, k):
        return remote(
            send_twin.at[far, k], got_twin.at[far, k], x_send.at[far, k], x_recv.at[far, k], twin
        )

    def y_copy(k):
        return remote(send_y.at[k], got_y.at[k], y_send.at[k], y_recv.at[k], across)

    def z_copy(k):
        return remote(
            send_z.at[k], got_z.at[k], z_send.at[k], z_recv.at[k],
            index_of(target(k), side, core),
        )

    def one_target(k, _):
        there = target(k)
        first, second = chunks(
            [index_of(there, 1 - side, 1 - core), index_of(there, side, 1 - core)]
        )
        send_twin[0, k] = first.astype(BF16)
        twin_copy(0, k).start()
        send_twin[1, k] = second.astype(BF16)
        twin_copy(1, k).start()
        first, second = chunks([index_of(there, 1 - side, core), index_of(there, side, core)])
        twin_copy(0, k).wait_recv()
        send_y[k] = (first + got_twin[0, k].astype(F32)).astype(BF16)
        y_copy(k).start()
        twin_copy(1, k).wait_recv()
        near[k] = second + got_twin[1, k].astype(F32)

        @pl.when(k > 0)
        def _():
            y_copy(k - 1).wait_recv()
            send_z[k - 1] = (near[k - 1] + got_y[k - 1].astype(F32)).astype(BF16)
            z_copy(k - 1).start()

        return 0

    lax.fori_loop(0, lines, one_target, 0)
    y_copy(lines - 1).wait_recv()
    for k in range(lines - 1):
        z_copy(k).wait_recv()
    for b in range(chunk // 8):
        cut = pl.ds(b * width, width)
        band = slice(b * 8, (b + 1) * 8)
        piece = near[lines - 1, band] + got_y[lines - 1, band].astype(F32)
        for k in range(lines - 1):
            piece += got_z[k, band].astype(F32)
        out[:, cut] = piece * cell_scaling(level[:, cut], label[:, cut], contrast, units)
    for copy in pending:
        copy.wait_send()
    for k in range(lines):
        twin_copy(0, k).wait_send()
        twin_copy(1, k).wait_send()
        y_copy(k).wait_send()
        if k < lines - 1:
            z_copy(k).wait_send()


def params(number):
    return pltpu.CompilerParams(
        collective_id=number, has_side_effects=True, vmem_limit_bytes=VMEM_LIMIT
    )


VM = pl.BlockSpec(memory_space=pltpu.VMEM)
SM = pl.BlockSpec(memory_space=pltpu.SMEM)
ANY = pl.BlockSpec(memory_space=pl.ANY)


def shards(
    probes,
    level_set,
    unit_label,
    contrast,
    station_weight,
    u_factor,
    v_factor,
    col_owner,
    col_local,
    row_owner,
    row_local,
    tile_rank,
):
    peers = lax.axis_size("tile")
    lines = peers // 4
    own_index = lax.axis_index("tile")
    tiles, rank_max, width = u_factor.shape
    cell_total = probes.shape[1]
    cell_blocks = cell_total // width
    station_blocks = station_weight.shape[0] // (peers * width)
    units = contrast.shape[0]
    half = width // 2
    parts = 4 if cell_blocks % 4 == 0 else 1
    dma = pltpu.SemaphoreType.DMA

    capacity = max(2, 2 * tiles // peers)
    size = min(GROUP, capacity)

    def own_part(table):
        return lax.dynamic_slice_in_dim(table.reshape(-1), own_index * tiles, tiles)

    owner, local = own_part(col_owner), own_part(col_local)
    row_who, row_where = own_part(row_owner), own_part(row_local)
    ranks = own_part(tile_rank)
    col_take = owner * cell_blocks + local
    row_take = row_who * station_blocks + row_where

    number = jnp.arange(tiles, dtype=jnp.int32)
    rank_bits = bits_of(rank_max + 1)

    def slots(owner, local, local_range, block, block_range):
        shift = rank_bits + bits_of(local_range)
        tile_shift = shift + bits_of(block_range)
        earlier = (owner[None, :] == owner[:, None]) & (number[None, :] < number[:, None])
        slot = owner * capacity + jnp.sum(earlier.astype(jnp.int32), axis=1)
        code = (number << tile_shift) | (block << shift) | (local << rank_bits) | ranks
        held = jnp.arange(peers * capacity, dtype=jnp.int32)[:, None] == slot[None, :]
        code = jnp.sum(jnp.where(held, code[None, :], 0), axis=1)
        rank = code & ((1 << rank_bits) - 1)
        where = (code >> rank_bits) & ((1 << (shift - rank_bits)) - 1)
        kept = jnp.arange(rank_max, dtype=jnp.int32)[None, :] < rank[:, None]
        lanes = jnp.where(kept, where[:, None], -1)
        lanes = lanes.reshape(peers * capacity // size, 1, size * rank_max)
        return code, lanes, (shift, tile_shift)

    row_codes, row_lanes, row_shifts = slots(
        row_who, row_where, station_blocks, col_take, peers * cell_blocks
    )
    col_codes, col_lanes, col_shifts = slots(
        owner, local, cell_blocks, row_take, peers * station_blocks
    )
    level = level_set.reshape(1, cell_total)
    label = unit_label.reshape(1, cell_total)
    weight = station_weight.reshape(1, -1)

    small = station_blocks * 8
    chunk = cell_blocks * 8
    pairs = peers // 2
    factors = pltpu.VMEM((tiles, rank_max, width), BF16)
    with jax.named_scope("hessian_kernel"):
        return pl.pallas_call(
            functools.partial(
                whole_kernel, lines, units, parts, capacity, rank_max, row_shifts, col_shifts
            ),
            out_shape=jax.ShapeDtypeStruct(probes.shape, F32),
            in_specs=[SM] * 3 + [VM] * 6 + [ANY] * 2,
            out_specs=VM,
            scratch_shapes=[
                factors,
                factors,
                pltpu.VMEM((peers * cell_blocks, 16, half), BF16),
                pltpu.VMEM((cell_blocks, 16, half), BF16),
                pltpu.VMEM((peers * station_blocks, 16, half), BF16),
                pltpu.VMEM((pairs, small, width), F32),
                pltpu.VMEM((pairs, small, width), F32),
                pltpu.VMEM((pairs, small, width), F32),
                pltpu.VMEM((pairs - 1, small, width), BF16),
                pltpu.VMEM((pairs - 1, small, width), BF16),
                pltpu.VMEM((station_blocks, 16, half), BF16),
                pltpu.VMEM((2, lines, chunk, width), BF16),
                pltpu.VMEM((2, lines, chunk, width), BF16),
                pltpu.VMEM((lines, chunk, width), BF16),
                pltpu.VMEM((lines, chunk, width), BF16),
                pltpu.VMEM((lines, chunk, width), F32),
                pltpu.VMEM((lines - 1, chunk, width), BF16),
                pltpu.VMEM((lines - 1, chunk, width), BF16),
                dma((pairs,)),
                dma((pairs,)),
                dma((pairs - 1,)),
                dma((pairs - 1,)),
                dma((pairs - 1,)),
                dma((pairs - 1,)),
                dma((pairs,)),
                dma((pairs,)),
                dma,
                dma,
                dma,
                dma((2, lines)),
                dma((2, lines)),
                dma((lines,)),
                dma((lines,)),
                dma((lines - 1,)),
                dma((lines - 1,)),
                dma,
            ]
            + gather_sems(lines, parts),
            compiler_params=params(0),
        )(
            contrast, row_codes, col_codes, row_lanes, col_lanes, probes, level, label, weight, u_factor, v_factor,
        )


def solution(mesh):
    placed = (
        P(None, ("groups", "tile")),
        P(("groups", "tile")),
        P(("groups", "tile")),
        P("groups"),
        P("groups"),
        P(("groups", "tile"), None, None),
        P(("groups", "tile"), None, None),
        P("groups", None),
        P("groups"),
        P("groups", None),
        P("groups"),
        P("groups"),
    )
    return jax.shard_map(
        shards, mesh=mesh, in_specs=placed, out_specs=P(None, ("groups", "tile")), check_vma=False
    )
```
